32 devices in a mesh: pts: 8 (over z, y), dp: 4 (over x, core).
Axes of the slice: x: 2, y: 2, z: 4, core: 2. Of those that a mesh axis runs over, the one named last changes fastest.
Arguments:
- features: bfloat16 [4, 8192, 256], P('dp', 'pts')
- hilbert_pos: int32 [4, 8192], P('dp', 'pts'), may hold values from 0 to 8191, as said below
- weight: bfloat16 [27, 256, 256], replicated, may hold values from -0.078125 to 0.078125
- neighbours: int32 [4, 16, 26], P('dp', 'pts'), may hold values from -1 to 15, as said below
- grad_out: bfloat16 [4, 8192, 256], P('dp', 'pts')
Outputs:
- conv_out: bfloat16 [4, 8192, 256], P('dp', 'pts')
- input_grad: bfloat16 [4, 8192, 256], P('dp', 'pts')
- weight_grad: bfloat16 [27, 256, 256], replicated
The draws below stay inside these ranges and needn't reach their ends.
Inputs may be any that keep to these rules, and one draw needn't show every extreme that they name: Each crop's row is a permutation of 0 to 8191. A point at row r goes to Hilbert owner hilbert_pos // 1024, and (owner - r // 1024 + 8 / 2) mod 8 is below 8. One device sends at most 256 points to one owner, exactly 256 to some owner in every crop; within a crop every device sends the same number of points to the owner k places ahead, for each k. Entries are block numbers within the same crop or -1. The relation is symmetric: h is the neighbour of g in direction d exactly when g is the neighbour of h in direction 25 - d. A neighbour h of g satisfies 1 <= |h - g| <= 2, and some block has a neighbour exactly 2 blocks away in every crop. A neighbour h > g lies in one of the directions 13 to 25; for each block and each t, at most one of its neighbours is t blocks ahead of it and at most one t blocks behind it.
All inputs are finite; a program needn't handle non-finite values.
Results may differ from the reference program's by a relative error of at most 0.0015.
Values may be sent and summed in bfloat16 or wider, within the bound.
No kernel may reach another device: no remote copies, remote signals or barrier semaphores. Data moves between devices by JAX's collectives and lax.ppermute only.
A program may use at most 128 MiB of HBM per device.

```python
import jax
import jax.numpy as jnp
import numpy as np
from jax import lax

C = 256
BLK_DEV = 2
PTS_DEV = 1024
CROPS = 4
NBLK = 16
NPTS = 8192
WIN = 8
N_PTS = 8


def shuffled(key_item):
    return jax.random.permutation(key_item, PTS_DEV)


def draw_features(key, part):
    own_key = jax.random.fold_in(key, 11)
    first, second = jax.random.split(own_key, 2)
    scales = 0.3 * 10.0 ** jax.random.uniform(first, (C,), jnp.float32)
    values = jnp.clip(jax.random.normal(second, (CROPS, NPTS, C), jnp.float32), -6.0, 6.0)
    return (values * scales).astype(jnp.bfloat16)


def draw_grad_out(key, part):
    own_key = jax.random.fold_in(key, 23)
    first, second = jax.random.split(own_key, 2)
    scales = 0.3 * 10.0 ** jax.random.uniform(first, (C,), jnp.float32)
    values = jnp.clip(jax.random.normal(second, (CROPS, NPTS, C), jnp.float32), -6.0, 6.0)
    return (values * scales).astype(jnp.bfloat16)


def draw_hilbert_pos(key, part):
    half_window = WIN // 2
    base_count = PTS_DEV // WIN
    crop_rows = []
    ranking = jnp.arange(PTS_DEV, dtype=jnp.int32)
    sources = jnp.arange(N_PTS, dtype=jnp.int32)
    for crop_index in range(CROPS):
        crop_key = jax.random.fold_in(key, crop_index)
        pairing = jax.random.permutation(jax.random.fold_in(crop_key, 1), WIN)
        moves = jax.random.randint(jax.random.fold_in(crop_key, 2), (half_window,), 0, base_count + 1)
        moves = moves.at[0].set(base_count)
        counts = jnp.full((WIN,), base_count, jnp.int32)
        counts = counts.at[pairing[0::2]].add(moves).at[pairing[1::2]].add(-moves)
        bounds = jnp.cumsum(counts)
        group = jnp.sum((ranking[:, None] >= bounds[None, :]).astype(jnp.int32), axis=1)
        owners = (sources[:, None] + group[None, :] - half_window) % N_PTS
        orders = jax.vmap(shuffled)(jax.random.split(jax.random.fold_in(crop_key, 3), N_PTS))
        places = jax.vmap(shuffled)(jax.random.split(jax.random.fold_in(crop_key, 4), N_PTS))
        values = owners * PTS_DEV + places[owners, ranking[None, :]]
        table = jnp.zeros((N_PTS, PTS_DEV), jnp.int32).at[sources[:, None], orders].set(values)
        crop_rows.append(table.reshape(NPTS))
    return jnp.stack(crop_rows)


def draw_neighbours(key, part):
    blocks = jnp.arange(NBLK, dtype=jnp.int32)
    labels = jnp.arange(26, dtype=jnp.int32)
    tables = []
    for crop_index in range(CROPS):
        crop_key = jax.random.fold_in(key, crop_index)
        order = jax.random.permutation(jax.random.fold_in(crop_key, 0), 13)
        neighbour_ids = jnp.full((NBLK, 26), -1, jnp.int32)
        for distance in range(1, BLK_DEV + 1):
            dist_key = jax.random.fold_in(crop_key, 100 + distance)
            choices_count = (13 - distance + BLK_DEV) // BLK_DEV
            pick = jax.random.randint(jax.random.fold_in(dist_key, 1), (NBLK,), 0, choices_count)
            label = 13 + order[distance - 1 + BLK_DEV * pick]
            alive = jax.random.randint(jax.random.fold_in(dist_key, 2), (NBLK,), 0, 4) > 0
            alive = (alive | (blocks == 0)) & (blocks + distance < NBLK)
            ahead = alive[:, None] & (labels[None, :] == label[:, None])
            neighbour_ids = jnp.where(ahead, blocks[:, None] + distance, neighbour_ids)
            back_label = jnp.concatenate([jnp.full((distance,), -1, jnp.int32), label[:-distance]])
            back_alive = jnp.concatenate([jnp.zeros((distance,), jnp.bool_), alive[:-distance]])
            behind = back_alive[:, None] & (labels[None, :] == 25 - back_label[:, None])
            neighbour_ids = jnp.where(behind, blocks[:, None] - distance, neighbour_ids)
        tables.append(neighbour_ids)
    return jnp.stack(tables)


def bell_draw(key, dims, width, bound, kind=jnp.bfloat16):
    result = width * jax.random.normal(key, dims, jnp.float32)
    return jnp.clip(result, min=-bound, max=bound).astype(kind)


def setup_inputs(seed: int = 0) -> dict:
    seeds = jax.random.split(jax.random.key(seed), 6)
    return {
        "features": draw_features(jax.random.fold_in(seeds[5], 71), 0),
        "hilbert_pos": draw_hilbert_pos(jax.random.fold_in(seeds[5], 71), 0),
        "weight": bell_draw(seeds[2], (27, C, C), (27 * C) ** -0.5, 0.078125),
        "neighbours": draw_neighbours(jax.random.fold_in(seeds[5], 71), 0),
        "grad_out": draw_grad_out(jax.random.fold_in(seeds[5], 71), 0),
    }


def offset_list():
    return [(a, b, c) for a in (-1, 0, 1) for b in (-1, 0, 1) for c in (-1, 0, 1)]

def side_values(sign, low_value, high_value, inner):
    if sign < 0:
        return [low_value]
    if sign > 0:
        return [high_value]
    return inner

def shell_tables():
    directions = [offset_item for offset_item in offset_list() if offset_item != (0, 0, 0)]
    shell_rows = []
    part_dir = []
    rim_cells = []
    starts = []
    for number, (a, b, c) in enumerate(directions):
        starts.append(len(shell_rows))
        for i in side_values(a, 0, 7, list(range(8))):
            for j in side_values(b, 0, 7, list(range(8))):
                for k in side_values(c, 0, 7, list(range(8))):
                    shell_rows.append(i * 64 + j * 8 + k)
                    part_dir.append(number)
        for i in side_values(a, 0, 9, list(range(1, 9))):
            for j in side_values(b, 0, 9, list(range(1, 9))):
                for k in side_values(c, 0, 9, list(range(1, 9))):
                    rim_cells.append(i * 100 + j * 10 + k)
    source_rows = [starts[25 - part_dir[m]] + m - starts[part_dir[m]] for m in range(len(part_dir))]
    grid_source = np.zeros(1000, np.int32)
    grid_source[np.array(rim_cells)] = 512 + np.arange(len(rim_cells))
    for i in range(8):
        for j in range(8):
            for k in range(8):
                grid_source[(i + 1) * 100 + (j + 1) * 10 + k + 1] = i * 64 + j * 8 + k
    return (np.array(shell_rows, np.int32), np.array(part_dir, np.int32), np.array(source_rows, np.int32), grid_source, np.array(rim_cells, np.int32))

def reference(features, hilbert_pos, weight, neighbours, grad_out):
    shell_rows, part_dir, source_rows, grid_source, rim_cells = shell_tables()
    rim_from = shell_rows[source_rows]
    channels = features.shape[-1]
    offsets = offset_list()
    block_count = features.shape[1] // 512
    conv_crops = []
    grad_crops = []
    weight_raw = jnp.zeros((27, channels, channels), jnp.float32)
    for crop_index in range(features.shape[0]):
        ordered = jnp.zeros_like(features[crop_index]).at[hilbert_pos[crop_index]].set(features[crop_index])
        neighbour_ids = neighbours[crop_index]
        cotangent = grad_out[crop_index]

        def grid_of(flat_rows, owners, block):
            start = (block * 512).astype(jnp.int32)
            center = lax.dynamic_slice_in_dim(flat_rows, start, 512, 0)
            present = owners >= 0
            gather_at = (jnp.where(present, owners, 0) * 512 + rim_from).astype(jnp.int32)
            rim_rows = jnp.where(present[:, None], flat_rows[gather_at], jnp.zeros((), flat_rows.dtype))
            whole = jnp.concatenate([center, rim_rows], axis=0)[grid_source]
            return (whole.reshape(10, 10, 10, channels), center)

        def one_block(carry, block):
            owners = neighbour_ids[block][part_dir]
            grid_x, center_x = grid_of(ordered, owners, block)
            grid_dy, center_dy = grid_of(cotangent, owners, block)
            forward = center_x.astype(jnp.float32)
            backward = center_dy.astype(jnp.float32)
            weight_terms = []
            for number, (a, b, c) in enumerate(offsets):
                moved = grid_x[1 + a:9 + a, 1 + b:9 + b, 1 + c:9 + c, :].reshape(512, channels)
                forward = forward + jnp.dot(moved, weight[number], preferred_element_type=jnp.float32)
                weight_terms.append(jnp.dot(moved.T, center_dy, preferred_element_type=jnp.float32))
                back_moved = grid_dy[1 - a:9 - a, 1 - b:9 - b, 1 - c:9 - c, :].reshape(512, channels)
                backward = backward + jnp.dot(back_moved, weight[number].T, preferred_element_type=jnp.float32)
            return (carry + jnp.stack(weight_terms), (forward.astype(jnp.bfloat16), backward.astype(jnp.bfloat16)))
        weight_raw, (conv_blocks, grad_blocks) = lax.scan(one_block, weight_raw, jnp.arange(block_count, dtype=jnp.int32))
        conv_crops.append(conv_blocks.reshape(-1, channels))
        grad_crops.append(grad_blocks.reshape(-1, channels))
    normalized = weight_raw / jnp.sqrt(jnp.mean(weight_raw * weight_raw) + 1e-06)
    return (jnp.stack(conv_crops), jnp.stack(grad_crops), normalized.astype(jnp.bfloat16))
```

```python
import functools

import jax
import jax.numpy as jnp
from jax import lax
from jax.experimental import pallas as pl
from jax.experimental.pallas import tpu as pltpu
from jax.sharding import PartitionSpec as P

BF = jnp.bfloat16
F32 = jnp.float32
I32 = jnp.int32
I16 = jnp.int16
C = 256
STEPS = (-2, -1, 1, 2)
HALF = 14
PART = 7
TAIL = 16
UNIT = PART * 16 + TAIL
TOP = 32760.0
MIB = 1 << 20


def dot(a, b):
    return lax.dot_general(a, b, (((1,), (0,)), ((), ())), preferred_element_type=F32)


def dot_nt(a, b):
    return lax.dot_general(a, b, (((1,), (1,)), ((), ())), preferred_element_type=F32)


def one_hot(index, key):
    return jnp.where(index == key, 1.0, 0.0).astype(BF)


def call(body, outs, args, smem=(), scratch=(), vmem=48, flops=0, moved=0):
    specs = [
        pl.BlockSpec(memory_space=pltpu.SMEM if i in smem else pltpu.VMEM)
        for i in range(len(args))
    ]
    shapes = [jax.ShapeDtypeStruct(s, d) for s, d in outs]
    return pl.pallas_call(
        body,
        out_shape=shapes,
        in_specs=specs,
        out_specs=[pl.BlockSpec(memory_space=pltpu.VMEM) for _ in shapes],
        scratch_shapes=list(scratch),
        compiler_params=pltpu.CompilerParams(vmem_limit_bytes=vmem * MIB),
        cost_estimate=pl.CostEstimate(flops=flops, bytes_accessed=moved, transcendentals=0),
    )(*args)


def pack_body(me_ref, pos_ref, x_ref, out_ref, *, count, window, cap, direct):
    rows = x_ref.shape[0]
    pos = pos_ref[...]
    owner = pos >> (rows.bit_length() - 1)
    local = pos & (rows - 1)
    if direct:
        chunk = owner
    else:
        chunk = (owner - me_ref[0] + window // 2) & (count - 1)
    member = (chunk == lax.broadcasted_iota(I32, (window, rows), 0)).astype(I32)
    lane = lax.broadcasted_iota(I32, (window, rows), 1)
    rank = member
    step = 1
    while step < rows:
        rank = rank + jnp.where(lane >= step, pltpu.roll(rank, step, 1), 0)
        step *= 2
    keys = jnp.where(member > 0, rank - 1, -1)
    line = lax.broadcasted_iota(I32, (TAIL, rows), 0)
    digits = jnp.where(line == 0, (local >> 5) + 1, jnp.where(line == 1, local & 31, 0))
    digits = digits.astype(F32).astype(BF)
    x = x_ref[...]
    slot = lax.broadcasted_iota(I32, (cap, rows), 0)
    for c in range(window):
        pick = one_hot(slot, keys[c : c + 1, :])
        out_ref[c, :cap, :] = dot(pick, x).astype(BF)
        tail = dot_nt(digits, pick)
        if cap < C:
            tail = jnp.concatenate([tail, jnp.zeros((TAIL, C - cap), F32)], axis=1)
        out_ref[c, cap : cap + TAIL, :] = tail.astype(BF)


def faces_of(rows_of, skey_ref, up_ref, down_ref, local_ref):
    slot = lax.broadcasted_iota(I32, (64, 512), 0)
    made = {}
    for g in range(2):
        rows = rows_of(g)
        pick = jnp.concatenate(
            [one_hot(slot, skey_ref[g * 4 + n : g * 4 + n + 1, :]) for n in range(4)], axis=0
        )
        face = dot(pick, rows).astype(BF)
        for n, t in enumerate(STEPS):
            made[g, t] = face[n * 64 : n * 64 + 64]
    for n, k in enumerate(((0, 2), (1, 1), (1, 2))):
        up_ref[n * 64 : n * 64 + 64, :] = made[k]
    for n, k in enumerate(((0, -1), (0, -2), (1, -2))):
        down_ref[n * 64 : n * 64 + 64, :] = made[k]
    for n, k in enumerate(((0, 1), (1, -1))):
        local_ref[n * 64 : n * 64 + 64, :] = made[k]


def faces_body(x_ref, skey_ref, up_ref, down_ref, local_ref):
    faces_of(lambda g: x_ref[g * 512 : g * 512 + 512, :], skey_ref, up_ref, down_ref, local_ref)


def order_body(got_ref, skey_ref, out_ref, up_ref, down_ref, local_ref, *, cap):
    chunks = got_ref.shape[0]
    rows = out_ref.shape[0]
    targets = []
    for c in range(chunks):
        tail = got_ref[c, cap : cap + TAIL, :].astype(F32)
        place = (tail[0:1] - 1.0) * 32.0 + tail[1:2]
        targets.append(place[:, :cap].astype(I32))
    for m in range(0, rows, 256):
        slot = lax.broadcasted_iota(I32, (256, cap), 0) + m
        total = jnp.zeros((256, C), F32)
        for c in range(chunks):
            total = total + dot(one_hot(slot, targets[c]), got_ref[c, :cap, :])
        out_ref[m : m + 256, :] = total.astype(BF)
    faces_of(lambda g: out_ref[g * 512 : g * 512 + 512, :], skey_ref, up_ref, down_ref, local_ref)


FACE_OUTS = [((192, C), BF), ((192, C), BF), ((128, C), BF)]


def fill_grid(block, x, pieces, ekey, grid_ref):
    wide = x.astype(F32)
    k_of = lax.broadcasted_iota(I32, (512, C), 0) & 7
    row = lax.broadcasted_iota(I32, (800, C), 0)
    cell = (row >> 3) * 10 + (row & 7) + 1
    for ci, c in enumerate((-1, 0, 1)):
        rim = dot(one_hot(cell, ekey - c), pieces)
        if c == 0:
            moved = wide
        elif c < 0:
            moved = jnp.where(k_of == 0, 0.0, pltpu.roll(wide, 1, 0))
        else:
            moved = jnp.where(k_of == 7, 0.0, pltpu.roll(wide, 511, 0))
        for i in range(10):
            stripe = rim[i * 80 : i * 80 + 80]
            if 1 <= i <= 8:
                inner = stripe[8:72] + moved[i * 64 - 64 : i * 64]
                stripe = jnp.concatenate([stripe[:8], inner, stripe[72:]], axis=0)
            for bi in range(3):
                grid_ref[block, bi * 3 + ci, i * 64 : i * 64 + 64, :] = stripe[
                    bi * 8 : bi * 8 + 64
                ].astype(BF)


def fill_grids(x_ref, up_ref, down_ref, local_ref, ekey_ref, grid_ref):
    def piece(ref, n):
        return ref[n * 64 : n * 64 + 64, :]

    sources = (
        (piece(up_ref, 0), piece(up_ref, 1), piece(local_ref, 1), piece(down_ref, 1)),
        (piece(up_ref, 2), piece(local_ref, 0), piece(down_ref, 0), piece(down_ref, 2)),
    )
    for g in range(2):
        fill_grid(
            g,
            x_ref[g * 512 : g * 512 + 512, :],
            jnp.concatenate(sources[g], axis=0),
            ekey_ref[g : g + 1, :],
            grid_ref,
        )


def convolve(x_ref, grid_ref, weight_ref, out_ref, acc_ref, flip):
    for g in range(2):
        acc_ref[g * 512 : g * 512 + 512, :] = x_ref[g * 512 : g * 512 + 512, :].astype(F32)

    def one(ab, carry):
        a, b = ab // 3, ab % 3
        start = pl.multiple_of(a * 64, 64)
        for g in range(2):
            total = acc_ref[g * 512 : g * 512 + 512, :]
            for c in range(3):
                rows = grid_ref[g, b * 3 + c, pl.ds(start, 512), :]
                if flip:
                    total = total + dot_nt(rows, weight_ref[26 - (ab * 3 + c)])
                else:
                    total = total + dot(rows, weight_ref[ab * 3 + c])
            acc_ref[g * 512 : g * 512 + 512, :] = total
        return carry

    lax.fori_loop(0, 9, one, 0)
    out_ref[...] = acc_ref[...].astype(BF)


def backward_body(x_ref, up, down, local, ekey, weight_ref, out_ref, turned_ref, grid_ref, acc_ref):
    fill_grids(x_ref, up, down, local, ekey, grid_ref)
    turned_ref[...] = x_ref[...].astype(F32).T.astype(BF)
    convolve(x_ref, grid_ref, weight_ref, out_ref, acc_ref, True)


def forward_body(x_ref, up, down, local, ekey, weight_ref, out_ref, grid_ref, acc_ref):
    fill_grids(x_ref, up, down, local, ekey, grid_ref)
    convolve(x_ref, grid_ref, weight_ref, out_ref, acc_ref, False)


GRID_SCRATCH = pltpu.VMEM((2, 9, 640, C), BF)


def scale_code(peak):
    peak = jnp.maximum(peak, 1e-30)
    power = jnp.floor(jnp.log2(peak))
    part = jnp.clip(jnp.ceil(peak * jnp.exp2(-power) * 64.0), 1.0, 200.0)
    return power * 256.0 + part


def scale_of(code):
    power = jnp.floor(code * (1.0 / 256.0))
    return jnp.exp2(power) * (code - power * 256.0) * (1.0 / 64.0)


def encode(values):
    code = scale_code(jnp.max(jnp.abs(values), axis=0, keepdims=True))
    return code, jnp.round(values * (TOP / scale_of(code))).astype(I32).astype(I16)


def decode(values, code):
    return values.astype(I32).astype(F32) * (scale_of(code) * (1.0 / TOP))


def tail_of(codes):
    lines = list(codes) + [jnp.zeros((1, C), F32)] * (TAIL - len(codes))
    return jnp.concatenate(lines, axis=0).astype(I32).astype(I16)


def tail_codes(ref, start):
    return ref[start : start + TAIL, :].astype(I32).astype(F32)


def kernel_grad_body(
    bits_ref, x_ref, up, down, local, ekey, turned_ref, own_ref, send_ref, grid_ref, code_ref
):
    fill_grids(x_ref, up, down, local, ekey, grid_ref)
    mine = bits_ref[0]

    def term(offset):
        at = jnp.minimum(offset, 26)
        a, bc = at // 9, at % 9
        start = pl.multiple_of(a * 64, 64)
        total = dot(turned_ref[:, :512], grid_ref[0, bc, pl.ds(start, 512), :])
        total = total + dot(turned_ref[:, 512:], grid_ref[1, bc, pl.ds(start, 512), :])
        return jnp.where(offset < 27, total, 0.0)

    code_ref[...] = jnp.zeros_like(code_ref)

    def send_one(i, carry):
        code, values = encode(term((1 - mine) * HALF + i))
        send_ref[pl.ds(pl.multiple_of(i * 256, 256), 256), :] = values
        code_ref[pl.ds(i, 1), :] = code
        return carry

    def keep_one(i, carry):
        own_ref[i] = term(mine * HALF + i)
        return carry

    lax.fori_loop(0, HALF, send_one, 0)
    send_ref[HALF * 256 :, :] = code_ref[...].astype(I32).astype(I16)
    lax.fori_loop(0, HALF, keep_one, 0)


def reduce_body(*refs, which, parts, rows):
    bits_ref, keep_ref, send_ref = refs[0], refs[-2], refs[-1]
    half = rows // 2
    mine = bits_ref[which]
    keep_at = pl.multiple_of(mine * half, half)
    send_at = pl.multiple_of((1 - mine) * half, half)
    codes = []
    for n, (first, many, total) in enumerate(parts):
        acc_ref, got_ref = refs[1 + 2 * n], refs[2 + 2 * n]
        tail = tail_codes(got_ref, total * rows)
        for i in range(first, first + many):
            at = len(codes)
            code = tail[i : i + 1]
            wide = acc_ref[i, pl.ds(send_at, half), :] + decode(
                got_ref[pl.ds(i * rows + send_at, half), :], code
            )
            new, values = encode(wide)
            codes.append(new)
            send_ref[at * half : at * half + half, :] = values
            keep_ref[at] = acc_ref[i, pl.ds(keep_at, half), :] + decode(
                got_ref[pl.ds(i * rows + keep_at, half), :], code
            )
    send_ref[len(codes) * half :, :] = tail_of(codes)


def reduce_step(bits, which, operands, parts, rows):
    many = sum(p[1] for p in parts)
    half = rows // 2
    outs = [((many, half, C), F32), ((many * half + TAIL, C), I16)]
    body = functools.partial(reduce_body, which=which, parts=parts, rows=rows)
    return call(body, outs, [bits, *operands], smem=(0,), moved=many * rows * C * 8)


def total_body(acc_ref, got_ref, out_ref):
    tail = tail_codes(got_ref, HALF * 16)
    for i in range(HALF):
        out_ref[i] = acc_ref[i] + decode(got_ref[i * 16 : i * 16 + 16, :], tail[i : i + 1])


def unit_body(total_ref, a_ref, b_ref):
    for p, out_ref in enumerate((a_ref, b_ref)):
        codes = []
        squares = jnp.zeros((1, C), F32)
        for i in range(PART):
            value = total_ref[p * PART + i]
            squares = squares + jnp.sum(value * value, axis=0, keepdims=True)
            code, coded = encode(value)
            codes.append(code)
            out_ref[i * 16 : i * 16 + 16, :] = coded
        squares = jnp.maximum(squares, 1e-30)
        power = jnp.floor(jnp.log2(squares))
        codes.append(power)
        codes.append(jnp.round(jnp.minimum(squares * jnp.exp2(-power) * 15000.0, 32000.0)))
        out_ref[PART * 16 :, :] = tail_of(codes)


def finish_body(bits_ref, own_a, own_b, far_a, far_b, out_ref, wide_ref, square_ref):
    mine = bits_ref[0]
    sides = ((mine, (own_a, own_b)), (1 - mine, (far_a, far_b)))

    def place_of(p, u):
        place = 0
        for n, which in enumerate(((1, 2, 3, 4), (2, 1, 3, 4))[p]):
            place = place * 2 + (bits_ref[which] ^ ((u >> (3 - n)) & 1))
        return place

    for half, refs in sides:
        for p in range(2):
            for u in range(16):
                tail = tail_codes(refs[p], u * UNIT + PART * 16)
                square_ref[pl.ds(half * 32 + p * 16 + place_of(p, u), 1), :] = (
                    jnp.exp2(tail[PART : PART + 1]) * tail[PART + 1 : PART + 2]
                )
    squares = jnp.sum(square_ref[...], axis=0, keepdims=True)
    mean = jnp.sum(squares, axis=1, keepdims=True) * (1.0 / (15000.0 * 27 * C * C))
    gain = 1.0 / jnp.sqrt(mean + 1e-06)
    for half, refs in sides:
        for p in range(2):
            places, scales = [], []
            for u in range(16):
                places.append(pl.multiple_of(place_of(p, u) * 16, 16))
                tail = tail_codes(refs[p], u * UNIT + PART * 16)
                scales.append(scale_of(tail[:8]) * gain * (1.0 / TOP))
            for i in range(PART):
                for u in range(16):
                    coded = refs[p][u * UNIT + i * 16 : u * UNIT + i * 16 + 16, :]
                    wide_ref[pl.ds(places[u], 16), :] = (
                        coded.astype(I32).astype(F32) * scales[u][i : i + 1]
                    )
                offset = half * HALF + p * PART + i

                @pl.when(offset < 27)
                def _():
                    out_ref[offset] = wide_ref[...].T.astype(BF)


def neighbour_keys(neighbours, first):
    blocks = neighbours.shape[0]
    own = first + lax.broadcasted_iota(I32, (blocks, 26), 0)
    lane = lax.broadcasted_iota(I32, (blocks, 26), 1)
    number = lane + (lane >= 13).astype(I32)
    found = []
    for t in STEPS:
        hit = (neighbours == own + t) & (neighbours >= 0)
        found.append(jnp.max(jnp.where(hit, number, -1), axis=1, keepdims=True))
    o = jnp.stack(found, axis=1)
    some = o >= 0
    o = jnp.maximum(o, 0)
    a, b, c = o // 9 - 1, (o // 3) % 3 - 1, o % 3 - 1
    fi, fj, fk = a == 0, b == 0, c == 0

    v = jnp.arange(512, dtype=I32)[None, None, :]
    i, j, k = v >> 6, (v >> 3) & 7, v & 7

    def at_face(step, coordinate):
        return (step == 0) | (coordinate == jnp.where(step > 0, 7, 0))

    on = some & at_face(a, i) & at_face(b, j) & at_face(c, k)
    rank = jnp.where(fi, i, 0)
    rank = rank * jnp.where(fj, 8, 1) + jnp.where(fj, j, 0)
    rank = rank * jnp.where(fk, 8, 1) + jnp.where(fk, k, 0)
    skey = jnp.where(on, rank, -1).reshape(blocks * 4, 512)

    m = jnp.arange(64, dtype=I32)[None, None, :]
    sk = jnp.where(fk, 3, 0)
    sj = jnp.where(fj, 3, 0)
    mk = m & ((1 << sk) - 1)
    mj = (m >> sk) & ((1 << sj) - 1)
    mi = m >> (sk + sj)
    inside = some & (mi < jnp.where(fi, 8, 1))

    def rim(step, free):
        return jnp.where(step == 0, free + 1, jnp.where(step > 0, 9, 0))

    cell = rim(a, mi) * 100 + rim(b, mj) * 10 + rim(c, mk)
    ekey = jnp.where(inside, cell, -100).reshape(blocks, 256)
    return skey, ekey


def swap(x, bit):
    axis, place = bit
    count = lax.axis_size(axis)
    return lax.ppermute(x, axis, [(i, i ^ (1 << place)) for i in range(count)])


def shift(x, step):
    count = lax.axis_size("pts")
    return lax.ppermute(
        x, "pts", [(i, i + step) for i in range(count) if 0 <= i + step < count]
    )


def device_bits():
    dp = lax.axis_size("dp").bit_length() - 1
    pts = lax.axis_size("pts").bit_length() - 1
    order = [("dp", n) for n in range(dp)] + [("pts", n) for n in range(pts)]
    return order[:5], order[5:]


def bit_value(bit):
    return (lax.axis_index(bit[0]) >> bit[1]) & 1


def on_device(features, hilbert_pos, weight, neighbours, grad_out):
    rows = features.shape[1]
    count = lax.axis_size("pts")
    me = lax.axis_index("pts").astype(I32)
    window = min(16, count)
    cap = 2 * rows // window
    direct = window == count
    split, extra = device_bits()
    bits = jnp.stack([bit_value(b) for b in split]).astype(I32)
    s0, s1, s2, s3, s4 = split

    body = functools.partial(pack_body, count=count, window=window, cap=cap, direct=direct)
    (packed,) = call(
        body,
        [((window, cap + TAIL, C), BF)],
        [me.reshape(1), hilbert_pos, features[0]],
        smem=(0,),
        flops=4 * rows * rows * C,
        moved=4 * rows * C * 2,
    )
    if direct:
        got = lax.all_to_all(packed, "pts", 0, 0, tiled=True)
    else:
        parts = []
        for w in range(window):
            step = w - window // 2
            turn = [(i, (i + step) % count) for i in range(count)]
            parts.append(packed[w] if step == 0 else lax.ppermute(packed[w], "pts", turn))
        got = jnp.stack(parts)

    skey, ekey = neighbour_keys(neighbours[0], me * (rows // 512))
    dy = grad_out[0]
    up, down, dy_local = call(faces_body, FACE_OUTS, [dy, skey], flops=4 * 512 * 256 * C)
    dy_up, dy_down = shift(up, 1), shift(down, -1)
    conv_flops = 2 * 27 * rows * C * C
    backward, turned = call(
        backward_body,
        [((rows, C), BF), ((C, rows), BF)],
        [dy, dy_up, dy_down, dy_local, ekey, weight],
        scratch=[GRID_SCRATCH, pltpu.VMEM((rows, C), F32)],
        flops=conv_flops,
        moved=6 * MIB,
    )

    x, up, down, x_local = call(
        functools.partial(order_body, cap=cap),
        [((rows, C), BF), *FACE_OUTS],
        [got, skey],
        flops=4 * rows * rows * C,
        moved=4 * rows * C * 2,
    )
    x_up, x_down = shift(up, 1), shift(down, -1)
    own, send = call(
        kernel_grad_body,
        [((HALF, C, C), F32), ((HALF * C + TAIL, C), I16)],
        [bits, x, x_up, x_down, x_local, ekey, turned],
        smem=(0,),
        scratch=[GRID_SCRATCH, pltpu.VMEM((TAIL, C), F32)],
        flops=conv_flops,
        moved=6 * MIB,
    )
    (forward,) = call(
        forward_body,
        [((rows, C), BF)],
        [x, x_up, x_down, x_local, ekey, weight],
        scratch=[GRID_SCRATCH, pltpu.VMEM((rows, C), F32)],
        flops=conv_flops,
        moved=6 * MIB,
    )

    came = swap(send, s0)
    keep_a, send_a = reduce_step(bits, 1, [own, came], ((0, PART, HALF),), 256)
    keep_b, send_b = reduce_step(bits, 2, [own, came], ((PART, PART, HALF),), 256)
    came_a, came_b = swap(send_a, s1), swap(send_b, s2)
    keep_a, send_a = reduce_step(bits, 2, [keep_a, came_a], ((0, PART, PART),), 128)
    keep_b, send_b = reduce_step(bits, 1, [keep_b, came_b], ((0, PART, PART),), 128)
    came_a, came_b = swap(send_a, s2), swap(send_b, s1)
    keep, send = reduce_step(
        bits, 3, [keep_a, came_a, keep_b, came_b], ((0, PART, PART), (0, PART, PART)), 64
    )
    came = swap(send, s3)
    keep, send = reduce_step(bits, 4, [keep, came], ((0, HALF, HALF),), 32)
    came = swap(send, s4)
    (total,) = call(total_body, [((HALF, 16, C), F32)], [keep, came])
    for b in extra:
        total = total + swap(total, b)
    unit_a, unit_b = call(unit_body, [((UNIT, C), I16), ((UNIT, C), I16)], [total])

    both = jnp.concatenate([unit_a, unit_b], axis=0)
    far = swap(both, s4)
    unit_a = jnp.concatenate([unit_a, far[:UNIT]], axis=0)
    unit_b = jnp.concatenate([unit_b, far[UNIT:]], axis=0)
    far = swap(jnp.concatenate([unit_a, unit_b], axis=0), s3)
    unit_a = jnp.concatenate([unit_a, far[: 2 * UNIT]], axis=0)
    unit_b = jnp.concatenate([unit_b, far[2 * UNIT :]], axis=0)
    far_a, far_b = swap(unit_a, s2), swap(unit_b, s1)
    unit_a = jnp.concatenate([unit_a, far_a], axis=0)
    unit_b = jnp.concatenate([unit_b, far_b], axis=0)
    far_a, far_b = swap(unit_a, s1), swap(unit_b, s2)
    unit_a = jnp.concatenate([unit_a, far_a], axis=0)
    unit_b = jnp.concatenate([unit_b, far_b], axis=0)
    far_a, far_b = swap(unit_a, s0), swap(unit_b, s0)
    (weight_grad,) = call(
        finish_body,
        [((27, C, C), BF)],
        [bits, unit_a, unit_b, far_a, far_b],
        smem=(0,),
        scratch=[pltpu.VMEM((C, C), F32), pltpu.VMEM((64, C), F32)],
    )
    return forward[None], backward[None], weight_grad


def solution(mesh):
    placed = (P("dp", "pts", None), P("dp", "pts"), P(), P("dp", "pts", None), P("dp", "pts", None))
    return jax.shard_map(
        on_device,
        mesh=mesh,
        in_specs=placed,
        out_specs=(P("dp", "pts", None), P("dp", "pts", None), P()),
        check_vma=False,
    )
```

```python
import functools

import jax
import jax.numpy as jnp
from jax import lax
from jax.experimental import pallas as pl
from jax.experimental.pallas import tpu as pltpu
from jax.sharding import PartitionSpec as P

BF = jnp.bfloat16
F32 = jnp.float32
I32 = jnp.int32
I16 = jnp.int16
C = 256
STEPS = (-2, -1, 1, 2)
HALF = 14
PART = 7
TAIL = 16
UNIT = PART * 16 + TAIL
TOP = 32760.0
MIB = 1 << 20


def dot(a, b):
    return lax.dot_general(a, b, (((1,), (0,)), ((), ())), preferred_element_type=F32)


def dot_nt(a, b):
    return lax.dot_general(a, b, (((1,), (1,)), ((), ())), preferred_element_type=F32)


def one_hot(index, key):
    return jnp.where(index == key, 1.0, 0.0).astype(BF)


def call(body, outs, args, smem=(), scratch=(), vmem=48, flops=0, moved=0):
    specs = [
        pl.BlockSpec(memory_space=pltpu.SMEM if i in smem else pltpu.VMEM)
        for i in range(len(args))
    ]
    shapes = [jax.ShapeDtypeStruct(s, d) for s, d in outs]
    return pl.pallas_call(
        body,
        out_shape=shapes,
        in_specs=specs,
        out_specs=[pl.BlockSpec(memory_space=pltpu.VMEM) for _ in shapes],
        scratch_shapes=list(scratch),
        compiler_params=pltpu.CompilerParams(vmem_limit_bytes=vmem * MIB),
        cost_estimate=pl.CostEstimate(flops=flops, bytes_accessed=moved, transcendentals=0),
    )(*args)


def links(near_ref, own, g):
    found = [jnp.int32(-1)] * 4
    for d in range(26):
        near = near_ref[g, d]
        for n, t in enumerate(STEPS):
            hit = jnp.logical_and(near >= 0, near == own + t)
            found[n] = jnp.where(hit, d + (d >= 13), found[n])
    return found


def key_rows(near_ref, own, g):
    v = lax.broadcasted_iota(I32, (1, 512), 1)
    i, j, k = v >> 6, (v >> 3) & 7, v & 7
    lane = lax.broadcasted_iota(I32, (1, 256), 1)
    m = lane & 63
    sends = []
    cells = jnp.full((1, 256), -100, I32)
    for n, o in enumerate(links(near_ref, own, g)):
        some = o >= 0
        o = jnp.maximum(o, 0)
        a, b, c = o // 9 - 1, (o // 3) % 3 - 1, o % 3 - 1
        sk = jnp.where(c == 0, 3, 0)
        sj = jnp.where(b == 0, 3, 0)
        rank = jnp.zeros((1, 512), I32)
        on = v >= jnp.where(some, 0, 512)
        for step, at, size in ((a, i, 3), (b, j, sj), (c, k, sk)):
            free = step == 0
            rank = (rank << jnp.where(free, 3, 0)) + at * jnp.where(free, 1, 0)
            low = jnp.where(free, 0, jnp.where(step > 0, 7, 0))
            high = jnp.where(free, 7, low)
            on = on & (at >= low) & (at <= high)
        sends.append(jnp.where(on, rank, -1))
        cell = jnp.zeros((1, 256), I32)
        for step, free_at in ((a, m >> (sk + sj)), (b, (m >> sk) & 7), (c, m & 7)):
            free = step == 0
            fixed = jnp.where(step > 0, 9, 0)
            cell = cell * 10 + (free_at + 1) * jnp.where(free, 1, 0) + jnp.where(free, 0, fixed)
        last = jnp.where(a == 0, 8, 1) << (sj + sk)
        inside = (lane >> 6 == n) & (m < jnp.where(some, last, 0))
        cells = jnp.where(inside, cell, cells)
    return sends, cells


def pack_body(me_ref, near_ref, pos_ref, x_ref, dy_ref, *refs, count, window, cap):
    *out_refs, skey_ref, ekey_ref, local_ref = refs
    rows = x_ref.shape[0]
    for g in range(2):
        sends, cells = key_rows(near_ref, me_ref[0] * 2 + g, g)
        for n in range(4):
            skey_ref[g * 4 + n : g * 4 + n + 1, :] = sends[n]
        ekey_ref[g : g + 1, :] = cells
    base = cap + TAIL
    faces_of(
        lambda g: dy_ref[g * 512 : g * 512 + 512, :],
        skey_ref,
        out_refs[window // 2 + 1].at[pl.ds(base, 192)],
        out_refs[window // 2 - 1].at[pl.ds(base, 192)],
        local_ref,
    )
    pos = pos_ref[...]
    owner = pos >> (rows.bit_length() - 1)
    local = pos & (rows - 1)
    chunk = (owner - me_ref[0] + window // 2) & (count - 1)
    member = (chunk == lax.broadcasted_iota(I32, (window, rows), 0)).astype(I32)
    lane = lax.broadcasted_iota(I32, (window, rows), 1)
    rank = member
    step = 1
    while step < rows:
        rank = rank + jnp.where(lane >= step, pltpu.roll(rank, step, 1), 0)
        step *= 2
    keys = jnp.where(member > 0, rank - 1, -1)
    line = lax.broadcasted_iota(I32, (TAIL, rows), 0)
    digits = jnp.where(line == 0, (local >> 5) + 1, jnp.where(line == 1, local & 31, 0))
    digits = digits.astype(F32).astype(BF)
    x = x_ref[...]
    slot = lax.broadcasted_iota(I32, (cap, rows), 0)
    for c in range(window):
        pick = one_hot(slot, keys[c : c + 1, :])
        out_refs[c][:cap, :] = dot(pick, x).astype(BF)
        tail = dot_nt(digits, pick)
        if cap < C:
            tail = jnp.concatenate([tail, jnp.zeros((TAIL, C - cap), F32)], axis=1)
        out_refs[c][cap : cap + TAIL, :] = tail.astype(BF)


def faces_of(rows_of, skey_ref, up_ref, down_ref, local_ref):
    slot = lax.broadcasted_iota(I32, (64, 512), 0)
    made = {}
    for g in range(2):
        rows = rows_of(g)
        pick = jnp.concatenate(
            [one_hot(slot, skey_ref[g * 4 + n : g * 4 + n + 1, :]) for n in range(4)], axis=0
        )
        face = dot(pick, rows).astype(BF)
        for n, t in enumerate(STEPS):
            made[g, t] = face[n * 64 : n * 64 + 64]
    for n, k in enumerate(((0, 2), (1, 1), (1, 2))):
        up_ref[n * 64 : n * 64 + 64, :] = made[k]
    for n, k in enumerate(((0, -1), (0, -2), (1, -2))):
        down_ref[n * 64 : n * 64 + 64, :] = made[k]
    for n, k in enumerate(((0, 1), (1, -1))):
        local_ref[n * 64 : n * 64 + 64, :] = made[k]


def order_body(*refs, cap):
    *got_refs, skey_ref, out_ref, up_ref, down_ref, local_ref = refs
    chunks = len(got_refs)
    rows = out_ref.shape[0]
    targets = []
    for c in range(chunks):
        tail = got_refs[c][cap : cap + TAIL, :].astype(F32)
        place = (tail[0:1] - 1.0) * 32.0 + tail[1:2]
        targets.append(place[:, :cap].astype(I32))
    for m in range(0, rows, 256):
        slot = lax.broadcasted_iota(I32, (256, cap), 0) + m
        total = jnp.zeros((256, C), F32)
        for c in range(chunks):
            total = total + dot(one_hot(slot, targets[c]), got_refs[c][:cap, :])
        out_ref[m : m + 256, :] = total.astype(BF)
    faces_of(lambda g: out_ref[g * 512 : g * 512 + 512, :], skey_ref, up_ref, down_ref, local_ref)


FACE_OUTS = [((192, C), BF), ((192, C), BF), ((128, C), BF)]


def fill_grid(block, x, pieces, ekey, grid_ref):
    wide = x.astype(F32)
    k_of = lax.broadcasted_iota(I32, (512, C), 0) & 7
    row = lax.broadcasted_iota(I32, (800, C), 0)
    cell = (row >> 3) * 10 + (row & 7) + 1
    for ci, c in enumerate((-1, 0, 1)):
        rim = dot(one_hot(cell, ekey - c), pieces)
        if c == 0:
            moved = wide
        elif c < 0:
            moved = jnp.where(k_of == 0, 0.0, pltpu.roll(wide, 1, 0))
        else:
            moved = jnp.where(k_of == 7, 0.0, pltpu.roll(wide, 511, 0))
        for i in range(10):
            stripe = rim[i * 80 : i * 80 + 80]
            if 1 <= i <= 8:
                inner = stripe[8:72] + moved[i * 64 - 64 : i * 64]
                stripe = jnp.concatenate([stripe[:8], inner, stripe[72:]], axis=0)
            grid_ref[block, ci, i * 80 : i * 80 + 80, :] = stripe.astype(BF)


def shifted(grid_ref, block, a, b, c):
    lines = []
    for i in range(8):
        start = (i + a) * 80 + b * 8
        if not isinstance(start, int):
            start = pl.multiple_of(start, 8)
        lines.append(grid_ref[block, c, pl.ds(start, 64), :])
    return jnp.concatenate(lines, axis=0)


def fill_grids(x_ref, up_ref, down_ref, local_ref, ekey_ref, grid_ref, base=0, blocks=(0, 1)):
    def piece(ref, n):
        start = n * 64 + (0 if ref is local_ref else base)
        return ref[start : start + 64, :]

    for at, g in enumerate(blocks):
        if g == 0:
            source = ((up_ref, 0), (up_ref, 1), (local_ref, 1), (down_ref, 1))
        else:
            source = ((up_ref, 2), (local_ref, 0), (down_ref, 0), (down_ref, 2))
        fill_grid(
            at,
            x_ref[g * 512 : g * 512 + 512, :],
            jnp.concatenate([piece(*p) for p in source], axis=0),
            ekey_ref[g : g + 1, :],
            grid_ref,
        )


def convolve(x_ref, grid_ref, weight_ref, out_ref, acc_ref, flip, blocks=(0, 1)):
    for at, g in enumerate(blocks):
        acc_ref[at * 512 : at * 512 + 512, :] = x_ref[g * 512 : g * 512 + 512, :].astype(F32)
    for ab in range(9):
        a, b = ab // 3, ab % 3
        for at, g in enumerate(blocks):
            total = acc_ref[at * 512 : at * 512 + 512, :]
            for c in range(3):
                rows = shifted(grid_ref, at, a, b, c)
                if flip:
                    total = total + dot_nt(rows, weight_ref[26 - (ab * 3 + c)])
                else:
                    total = total + dot(rows, weight_ref[ab * 3 + c])
            acc_ref[at * 512 : at * 512 + 512, :] = total
    for at, g in enumerate(blocks):
        out_ref[g * 512 : g * 512 + 512, :] = acc_ref[at * 512 : at * 512 + 512, :].astype(BF)


def turn_body(x_ref, out_ref):
    out_ref[...] = x_ref[...].astype(F32).T.astype(BF)


def backward_first_body(x, up, down, local, ekey, weight_ref, out_ref, grid_ref, acc_ref, *, base):
    fill_grids(x, up, down, local, ekey, grid_ref, base, (0,))
    convolve(x, grid_ref, weight_ref, out_ref, acc_ref, True, (0,))


def backward_body(x, up, down, local, ekey, weight_ref, first_ref, out_ref, grid_ref, acc_ref, *, base):
    fill_grids(x, up, down, local, ekey, grid_ref, base, (1,))
    out_ref[:512, :] = first_ref[...]
    convolve(x, grid_ref, weight_ref, out_ref, acc_ref, True, (1,))


def forward_body(x_ref, grid_ref, weight_ref, out_ref, acc_ref):
    convolve(x_ref, grid_ref, weight_ref, out_ref, acc_ref, False)


GRID = (2, 3, 800, C)


def scale_code(peak):
    peak = jnp.maximum(peak, 1e-30)
    power = jnp.floor(jnp.log2(peak))
    part = jnp.clip(jnp.ceil(peak * jnp.exp2(-power) * 64.0), 1.0, 200.0)
    return power * 256.0 + part


def scale_of(code):
    power = jnp.floor(code * (1.0 / 256.0))
    return jnp.exp2(power) * (code - power * 256.0) * (1.0 / 64.0)


def encode(values):
    code = scale_code(jnp.max(jnp.abs(values), axis=0, keepdims=True))
    return code, jnp.round(values * (TOP / scale_of(code))).astype(I32).astype(I16)


def decode(values, code):
    return values.astype(I32).astype(F32) * (scale_of(code) * (1.0 / TOP))


def tail_of(codes):
    lines = list(codes) + [jnp.zeros((1, C), F32)] * (TAIL - len(codes))
    return jnp.concatenate(lines, axis=0).astype(I32).astype(I16)


def tail_codes(ref, start):
    return ref[start : start + TAIL, :].astype(I32).astype(F32)


def term(grid_ref, turned_ref, offset):
    at = jnp.minimum(offset, 26)
    a, b, c = at // 9, (at // 3) % 3, at % 3
    total = dot(turned_ref[:, :512], shifted(grid_ref, 0, a, b, c))
    total = total + dot(turned_ref[:, 512:], shifted(grid_ref, 1, a, b, c))
    return jnp.where(offset < 27, total, 0.0)


def send_terms(bits_ref, grid_ref, turned_ref, send_ref, first):
    codes = []
    for i in range(PART):
        offset = (1 - bits_ref[0]) * HALF + first + i
        code, values = encode(term(grid_ref, turned_ref, offset))
        codes.append(code)
        send_ref[i * 256 : i * 256 + 256, :] = values
    send_ref[PART * 256 :, :] = tail_of(codes)


def first_terms_body(bits_ref, x, up, down, local, ekey, turned_ref, grid_ref, send_ref):
    fill_grids(x, up, down, local, ekey, grid_ref)
    send_terms(bits_ref, grid_ref, turned_ref, send_ref, 0)


def more_terms_body(bits_ref, grid_ref, turned_ref, send_ref):
    send_terms(bits_ref, grid_ref, turned_ref, send_ref, PART)


def own_terms_body(bits_ref, grid_ref, turned_ref, got_ref, keep_ref, send_ref, *, first, which):
    tail = tail_codes(got_ref, PART * 256)
    upper = bits_ref[which] > 0
    codes = []
    for i in range(PART):
        total = term(grid_ref, turned_ref, bits_ref[0] * HALF + first + i)
        total = total + decode(got_ref[i * 256 : i * 256 + 256, :], tail[i : i + 1])
        keep_ref[i] = jnp.where(upper, total[128:], total[:128])
        code, values = encode(jnp.where(upper, total[:128], total[128:]))
        codes.append(code)
        send_ref[i * 128 : i * 128 + 128, :] = values
    send_ref[PART * 128 :, :] = tail_of(codes)


def reduce_body(*refs, which, parts, rows):
    bits_ref, keep_ref, send_ref = refs[0], refs[-2], refs[-1]
    half = rows // 2
    mine = bits_ref[which]
    keep_at = pl.multiple_of(mine * half, half)
    send_at = pl.multiple_of((1 - mine) * half, half)
    codes = []
    for n, (first, many, total) in enumerate(parts):
        acc_ref, got_ref = refs[1 + 2 * n], refs[2 + 2 * n]
        tail = tail_codes(got_ref, total * rows)
        for i in range(first, first + many):
            at = len(codes)
            code = tail[i : i + 1]
            wide = acc_ref[i, pl.ds(send_at, half), :] + decode(
                got_ref[pl.ds(i * rows + send_at, half), :], code
            )
            new, values = encode(wide)
            codes.append(new)
            send_ref[at * half : at * half + half, :] = values
            keep_ref[at] = acc_ref[i, pl.ds(keep_at, half), :] + decode(
                got_ref[pl.ds(i * rows + keep_at, half), :], code
            )
    send_ref[len(codes) * half :, :] = tail_of(codes)


def reduce_step(bits, which, operands, parts, rows):
    many = sum(p[1] for p in parts)
    half = rows // 2
    outs = [((many, half, C), F32), ((many * half + TAIL, C), I16)]
    body = functools.partial(reduce_body, which=which, parts=parts, rows=rows)
    return call(body, outs, [bits, *operands], smem=(0,), moved=many * rows * C * 8)


def total_body(acc_ref, got_ref, out_ref):
    tail = tail_codes(got_ref, HALF * 16)
    for i in range(HALF):
        out_ref[i] = acc_ref[i] + decode(got_ref[i * 16 : i * 16 + 16, :], tail[i : i + 1])


def unit_body(total_ref, a_ref, b_ref):
    for p, out_ref in enumerate((a_ref, b_ref)):
        codes = []
        squares = jnp.zeros((1, C), F32)
        for i in range(PART):
            value = total_ref[p * PART + i]
            squares = squares + jnp.sum(value * value, axis=0, keepdims=True)
            code, coded = encode(value)
            codes.append(code)
            out_ref[i * 16 : i * 16 + 16, :] = coded
        squares = jnp.maximum(squares, 1e-30)
        power = jnp.floor(jnp.log2(squares))
        codes.append(power)
        codes.append(jnp.round(jnp.minimum(squares * jnp.exp2(-power) * 15000.0, 32000.0)))
        out_ref[PART * 16 :, :] = tail_of(codes)


def finish_body(bits_ref, *refs):
    out_ref, wide_ref, square_ref = refs[8:]
    mine = bits_ref[0]
    halves = (mine, 1 - mine)

    def place_of(p, u):
        place = 0
        for n, which in enumerate(((1, 2, 3, 4), (2, 1, 3, 4))[p]):
            place = place * 2 + (bits_ref[which] ^ ((u >> (3 - n)) & 1))
        return place

    def ref_of(side, p, u):
        return refs[side * 4 + p * 2 + u // 8], (u % 8) * UNIT

    for side in range(2):
        for p in range(2):
            for u in range(16):
                ref, at = ref_of(side, p, u)
                tail = tail_codes(ref, at + PART * 16)
                square_ref[pl.ds(halves[side] * 32 + p * 16 + place_of(p, u), 1), :] = (
                    jnp.exp2(tail[PART : PART + 1]) * tail[PART + 1 : PART + 2]
                )
    squares = jnp.sum(square_ref[...], axis=0, keepdims=True)
    mean = jnp.sum(squares, axis=1, keepdims=True) * (1.0 / (15000.0 * 27 * C * C))
    gain = 1.0 / jnp.sqrt(mean + 1e-06)
    for side in range(2):
        for p in range(2):
            places, scales = [], []
            for u in range(16):
                ref, at = ref_of(side, p, u)
                places.append(pl.multiple_of(place_of(p, u) * 16, 16))
                scales.append(scale_of(tail_codes(ref, at + PART * 16)[:8]) * gain * (1.0 / TOP))
            for i in range(PART):
                for u in range(16):
                    ref, at = ref_of(side, p, u)
                    coded = ref[at + i * 16 : at + i * 16 + 16, :]
                    wide_ref[i % 2, pl.ds(places[u], 16), :] = (
                        coded.astype(I32).astype(F32) * scales[u][i : i + 1]
                    ).astype(BF)
                offset = halves[side] * HALF + p * PART + i

                @pl.when(offset < 27)
                def _():
                    out_ref[offset] = wide_ref[i % 2].T


def swap(x, bit):
    axis, place = bit
    count = lax.axis_size(axis)
    return lax.ppermute(x, axis, [(i, i ^ (1 << place)) for i in range(count)])


def shift(x, step):
    count = lax.axis_size("pts")
    return lax.ppermute(
        x, "pts", [(i, i + step) for i in range(count) if 0 <= i + step < count]
    )


def device_bits():
    dp = lax.axis_size("dp").bit_length() - 1
    pts = lax.axis_size("pts").bit_length() - 1
    order = [("dp", n) for n in range(dp)] + [("pts", n) for n in range(pts)]
    return order[:5], order[5:]


def bit_value(bit):
    return (lax.axis_index(bit[0]) >> bit[1]) & 1


def on_device(features, hilbert_pos, weight, neighbours, grad_out):
    rows = features.shape[1]
    count = lax.axis_size("pts")
    me = lax.axis_index("pts").astype(I32)
    window = min(16, count)
    cap = 2 * rows // window
    split, extra = device_bits()
    bits = jnp.stack([bit_value(b) for b in split]).astype(I32)
    s0, s1, s2, s3, s4 = split

    dy = grad_out[0]
    lines = [cap + TAIL + (192 if abs(w - window // 2) == 1 else 0) for w in range(window)]
    *packed, skey, ekey, dy_local = call(
        functools.partial(pack_body, count=count, window=window, cap=cap),
        [*(((n, C), BF) for n in lines), ((8, 512), I32), ((2, C), I32), ((128, C), BF)],
        [me.reshape(1), neighbours[0], hilbert_pos, features[0], dy],
        smem=(0, 1),
        flops=4 * rows * rows * C,
        moved=4 * rows * C * 2,
    )
    got = [None] * window
    for w in sorted(range(window), key=lambda w: (-abs(w - window // 2), w)):
        step = w - window // 2
        turn = [(i, (i + step) % count) for i in range(count)]
        got[w] = packed[w] if step == 0 else lax.ppermute(packed[w], "pts", turn)

    conv_flops = 2 * 27 * rows * C * C
    part_flops = conv_flops // 4
    (turned,) = call(turn_body, [((C, rows), BF)], [dy])

    x, up, down, x_local = call(
        functools.partial(order_body, cap=cap),
        [((rows, C), BF), *FACE_OUTS],
        [*got, skey],
        flops=4 * rows * rows * C,
        moved=4 * rows * C * 2,
    )
    x_up, x_down = shift(up, 1), shift(down, -1)
    grid, send_a = call(
        first_terms_body,
        [(GRID, BF), ((PART * C + TAIL, C), I16)],
        [bits, x, x_up, x_down, x_local, ekey, turned],
        smem=(0,),
        flops=part_flops,
        moved=5 * MIB,
    )
    came_a = swap(send_a, s0)
    (send_b,) = call(
        more_terms_body,
        [((PART * C + TAIL, C), I16)],
        [bits, grid, turned],
        smem=(0,),
        flops=part_flops,
        moved=5 * MIB,
    )
    came_b = swap(send_b, s0)
    own_outs = [((PART, 128, C), F32), ((PART * 128 + TAIL, C), I16)]
    keep_a, send_a = call(
        functools.partial(own_terms_body, first=0, which=1),
        own_outs,
        [bits, grid, turned, came_a],
        smem=(0,),
        flops=part_flops,
        moved=5 * MIB,
    )
    came_a = swap(send_a, s1)
    keep_b, send_b = call(
        functools.partial(own_terms_body, first=PART, which=2),
        own_outs,
        [bits, grid, turned, came_b],
        smem=(0,),
        flops=part_flops,
        moved=5 * MIB,
    )
    came_b = swap(send_b, s2)
    x, grid, keep_b = lax.optimization_barrier((x, grid, keep_b))
    (forward,) = call(
        forward_body,
        [((rows, C), BF)],
        [x, grid, weight],
        scratch=[pltpu.VMEM((rows, C), F32)],
        flops=conv_flops,
        moved=6 * MIB,
    )
    forward, came_a, came_b = lax.optimization_barrier((forward, came_a, came_b))

    keep_a, send_a = reduce_step(bits, 2, [keep_a, came_a], ((0, PART, PART),), 128)
    keep_b, send_b = reduce_step(bits, 1, [keep_b, came_b], ((0, PART, PART),), 128)
    came_a, came_b = swap(send_a, s2), swap(send_b, s1)
    keep, send = reduce_step(
        bits, 3, [keep_a, came_a, keep_b, came_b], ((0, PART, PART), (0, PART, PART)), 64
    )
    came = swap(send, s3)
    keep, send = reduce_step(bits, 4, [keep, came], ((0, HALF, HALF),), 32)
    came = swap(send, s4)
    (total,) = call(total_body, [((HALF, 16, C), F32)], [keep, came])
    for b in extra:
        total = total + swap(total, b)
    unit_a, unit_b = call(unit_body, [((UNIT, C), I16), ((UNIT, C), I16)], [total])

    unit_a, unit_b, dy = lax.optimization_barrier((unit_a, unit_b, dy))
    back_args = [got[window // 2 + 1], got[window // 2 - 1], dy_local, ekey, weight]
    back_scratch = [pltpu.VMEM((1, 3, 800, C), BF), pltpu.VMEM((512, C), F32)]
    far = swap(jnp.concatenate([unit_a, unit_b], axis=0), s4)
    (backward,) = call(
        functools.partial(backward_first_body, base=cap + TAIL),
        [((512, C), BF)],
        [dy, *back_args],
        scratch=back_scratch,
        flops=conv_flops // 2,
        moved=5 * MIB,
    )
    far, backward, dy = lax.optimization_barrier((far, backward, dy))
    unit_a = jnp.concatenate([unit_a, far[:UNIT]], axis=0)
    unit_b = jnp.concatenate([unit_b, far[UNIT:]], axis=0)
    far = swap(jnp.concatenate([unit_a, unit_b], axis=0), s3)
    (backward,) = call(
        functools.partial(backward_body, base=cap + TAIL),
        [((rows, C), BF)],
        [dy, *back_args, backward],
        scratch=back_scratch,
        flops=conv_flops // 2,
        moved=5 * MIB,
    )
    far, backward = lax.optimization_barrier((far, backward))
    unit_a = jnp.concatenate([unit_a, far[: 2 * UNIT]], axis=0)
    unit_b = jnp.concatenate([unit_b, far[2 * UNIT :]], axis=0)
    far_a, far_b = swap(unit_a, s2), swap(unit_b, s1)
    unit_a = jnp.concatenate([unit_a, far_a], axis=0)
    unit_b = jnp.concatenate([unit_b, far_b], axis=0)
    far_a, far_b = swap(unit_a, s1), swap(unit_b, s2)
    other_a, other_b = swap(unit_a, s0), swap(unit_b, s0)
    other_far_a, other_far_b = swap(far_a, s0), swap(far_b, s0)
    (weight_grad,) = call(
        finish_body,
        [((27, C, C), BF)],
        [bits, unit_a, far_a, unit_b, far_b, other_a, other_far_a, other_b, other_far_b],
        smem=(0,),
        scratch=[pltpu.VMEM((2, C, C), BF), pltpu.VMEM((64, C), F32)],
    )
    return forward[None], backward[None], weight_grad


def solution(mesh):
    placed = (P("dp", "pts", None), P("dp", "pts"), P(), P("dp", "pts", None), P("dp", "pts", None))
    return jax.shard_map(
        on_device,
        mesh=mesh,
        in_specs=placed,
        out_specs=(P("dp", "pts", None), P("dp", "pts", None), P()),
        check_vma=False,
    )
```

```python
import functools

import jax
import jax.numpy as jnp
from jax import lax
from jax.experimental import pallas as pl
from jax.experimental.pallas import tpu as pltpu
from jax.sharding import PartitionSpec as P

BF = jnp.bfloat16
F32 = jnp.float32
I32 = jnp.int32
I16 = jnp.int16
C = 256
STEPS = (-2, -1, 1, 2)
HALF = 14
PART = 7
TAIL = 16
UNIT = PART * 16 + TAIL
TOP = 32760.0
MIB = 1 << 20


def dot(a, b):
    return lax.dot_general(a, b, (((1,), (0,)), ((), ())), preferred_element_type=F32)


def dot_nt(a, b):
    return lax.dot_general(a, b, (((1,), (1,)), ((), ())), preferred_element_type=F32)


def one_hot(index, key):
    return jnp.where(index == key, 1.0, 0.0).astype(BF)


def call(body, outs, args, smem=(), scratch=(), vmem=48, flops=0, moved=0, far=(), far_out=False):
    specs = [
        pl.BlockSpec(
            memory_space=pltpu.HBM if i in far else pltpu.SMEM if i in smem else pltpu.VMEM
        )
        for i in range(len(args))
    ]
    shapes = [jax.ShapeDtypeStruct(s, d) for s, d in outs]
    return pl.pallas_call(
        body,
        out_shape=shapes,
        in_specs=specs,
        out_specs=[
            pl.BlockSpec(memory_space=pltpu.HBM if far_out else pltpu.VMEM) for _ in shapes
        ],
        scratch_shapes=list(scratch),
        compiler_params=pltpu.CompilerParams(vmem_limit_bytes=vmem * MIB),
        cost_estimate=pl.CostEstimate(flops=flops, bytes_accessed=moved, transcendentals=0),
    )(*args)


def links(near_ref, own, g):
    found = [jnp.int32(-1)] * 4
    for d in range(26):
        near = near_ref[g, d]
        for n, t in enumerate(STEPS):
            hit = jnp.logical_and(near >= 0, near == own + t)
            found[n] = jnp.where(hit, d + (d >= 13), found[n])
    return found


def key_rows(near_ref, own, g):
    v = lax.broadcasted_iota(I32, (1, 512), 1)
    i, j, k = v >> 6, (v >> 3) & 7, v & 7
    lane = lax.broadcasted_iota(I32, (1, 256), 1)
    m = lane & 63
    sends = []
    cells = jnp.full((1, 256), -100, I32)
    for n, o in enumerate(links(near_ref, own, g)):
        some = o >= 0
        o = jnp.maximum(o, 0)
        a, b, c = o // 9 - 1, (o // 3) % 3 - 1, o % 3 - 1
        sk = jnp.where(c == 0, 3, 0)
        sj = jnp.where(b == 0, 3, 0)
        rank = jnp.zeros((1, 512), I32)
        on = v >= jnp.where(some, 0, 512)
        for step, at, size in ((a, i, 3), (b, j, sj), (c, k, sk)):
            free = step == 0
            rank = (rank << jnp.where(free, 3, 0)) + at * jnp.where(free, 1, 0)
            low = jnp.where(free, 0, jnp.where(step > 0, 7, 0))
            high = jnp.where(free, 7, low)
            on = on & (at >= low) & (at <= high)
        sends.append(jnp.where(on, rank, -1))
        cell = jnp.zeros((1, 256), I32)
        for step, free_at in ((a, m >> (sk + sj)), (b, (m >> sk) & 7), (c, m & 7)):
            free = step == 0
            fixed = jnp.where(step > 0, 9, 0)
            cell = cell * 10 + (free_at + 1) * jnp.where(free, 1, 0) + jnp.where(free, 0, fixed)
        last = jnp.where(a == 0, 8, 1) << (sj + sk)
        inside = (lane >> 6 == n) & (m < jnp.where(some, last, 0))
        cells = jnp.where(inside, cell, cells)
    return sends, cells


def pack_body(me_ref, *refs, count, window, cap):
    sources, refs = refs[:4], refs[4:]
    *out_refs, skey_ref, ekey_ref, local_ref = refs[: window + 3]
    *landed, sem = refs[window + 3 :]
    copies = [
        pltpu.make_async_copy(source, to, sem.at[n])
        for n, (source, to) in enumerate(zip(sources, landed, strict=True))
    ]
    for copy in copies:
        copy.start()
    near_ref, pos_ref, dy_ref, x_ref = landed
    rows = x_ref.shape[0]
    copies[0].wait()
    for g in range(2):
        sends, cells = key_rows(near_ref, me_ref[0] * 2 + g, g)
        for n in range(4):
            skey_ref[g * 4 + n : g * 4 + n + 1, :] = sends[n]
        ekey_ref[g : g + 1, :] = cells
    copies[1].wait()
    copies[2].wait()
    base = cap + TAIL
    faces_of(
        lambda g: dy_ref[g * 512 : g * 512 + 512, :],
        skey_ref,
        out_refs[window // 2 + 1].at[pl.ds(base, 192)],
        out_refs[window // 2 - 1].at[pl.ds(base, 192)],
        local_ref,
    )
    pos = pos_ref[...]
    owner = pos >> (rows.bit_length() - 1)
    local = pos & (rows - 1)
    chunk = (owner - me_ref[0] + window // 2) & (count - 1)
    member = (chunk == lax.broadcasted_iota(I32, (window, rows), 0)).astype(I32)
    lane = lax.broadcasted_iota(I32, (window, rows), 1)
    rank = member
    step = 1
    while step < rows:
        rank = rank + jnp.where(lane >= step, pltpu.roll(rank, step, 1), 0)
        step *= 2
    keys = jnp.where(member > 0, rank - 1, -1)
    line = lax.broadcasted_iota(I32, (TAIL, rows), 0)
    digits = jnp.where(line == 0, (local >> 5) + 1, jnp.where(line == 1, local & 31, 0))
    digits = digits.astype(F32).astype(BF)
    copies[3].wait()
    x = x_ref[...]
    slot = lax.broadcasted_iota(I32, (cap, rows), 0)
    for c in range(window):
        pick = one_hot(slot, keys[c : c + 1, :])
        out_refs[c][:cap, :] = dot(pick, x).astype(BF)
        tail = dot_nt(digits, pick)
        if cap < C:
            tail = jnp.concatenate([tail, jnp.zeros((TAIL, C - cap), F32)], axis=1)
        out_refs[c][cap : cap + TAIL, :] = tail.astype(BF)


def faces_of(rows_of, skey_ref, up_ref, down_ref, local_ref):
    slot = lax.broadcasted_iota(I32, (64, 512), 0)
    made = {}
    for g in range(2):
        rows = rows_of(g)
        pick = jnp.concatenate(
            [one_hot(slot, skey_ref[g * 4 + n : g * 4 + n + 1, :]) for n in range(4)], axis=0
        )
        face = dot(pick, rows).astype(BF)
        for n, t in enumerate(STEPS):
            made[g, t] = face[n * 64 : n * 64 + 64]
    for n, k in enumerate(((0, 2), (1, 1), (1, 2))):
        up_ref[n * 64 : n * 64 + 64, :] = made[k]
    for n, k in enumerate(((0, -1), (0, -2), (1, -2))):
        down_ref[n * 64 : n * 64 + 64, :] = made[k]
    for n, k in enumerate(((0, 1), (1, -1))):
        local_ref[n * 64 : n * 64 + 64, :] = made[k]


def order_body(*refs, cap):
    *got_refs, skey_ref, out_ref, up_ref, down_ref, local_ref = refs
    chunks = len(got_refs)
    rows = out_ref.shape[0]
    targets = []
    for c in range(chunks):
        tail = got_refs[c][cap : cap + TAIL, :].astype(F32)
        place = (tail[0:1] - 1.0) * 32.0 + tail[1:2]
        targets.append(place[:, :cap].astype(I32))
    for m in range(0, rows, 256):
        slot = lax.broadcasted_iota(I32, (256, cap), 0) + m
        total = jnp.zeros((256, C), F32)
        for c in range(chunks):
            total = total + dot(one_hot(slot, targets[c]), got_refs[c][:cap, :])
        out_ref[m : m + 256, :] = total.astype(BF)
    faces_of(lambda g: out_ref[g * 512 : g * 512 + 512, :], skey_ref, up_ref, down_ref, local_ref)


FACE_OUTS = [((192, C), BF), ((192, C), BF), ((128, C), BF)]


def fill_grid(block, x, pieces, ekey, grid_ref):
    wide = x.astype(F32)
    k_of = lax.broadcasted_iota(I32, (512, C), 0) & 7
    row = lax.broadcasted_iota(I32, (800, C), 0)
    cell = (row >> 3) * 10 + (row & 7) + 1
    for ci, c in enumerate((-1, 0, 1)):
        rim = dot(one_hot(cell, ekey - c), pieces)
        if c == 0:
            moved = wide
        elif c < 0:
            moved = jnp.where(k_of == 0, 0.0, pltpu.roll(wide, 1, 0))
        else:
            moved = jnp.where(k_of == 7, 0.0, pltpu.roll(wide, 511, 0))
        for i in range(10):
            stripe = rim[i * 80 : i * 80 + 80]
            if 1 <= i <= 8:
                inner = stripe[8:72] + moved[i * 64 - 64 : i * 64]
                stripe = jnp.concatenate([stripe[:8], inner, stripe[72:]], axis=0)
            grid_ref[block, ci, i * 80 : i * 80 + 80, :] = stripe.astype(BF)


def shifted(grid_ref, block, a, b, c):
    lines = []
    for i in range(8):
        start = (i + a) * 80 + b * 8
        if not isinstance(start, int):
            start = pl.multiple_of(start, 8)
        lines.append(grid_ref[block, c, pl.ds(start, 64), :])
    return jnp.concatenate(lines, axis=0)


def fill_grids(x_ref, up_ref, down_ref, local_ref, ekey_ref, grid_ref, base=0, blocks=(0, 1)):
    def piece(ref, n):
        start = n * 64 + (0 if ref is local_ref else base)
        return ref[start : start + 64, :]

    for at, g in enumerate(blocks):
        if g == 0:
            source = ((up_ref, 0), (up_ref, 1), (local_ref, 1), (down_ref, 1))
        else:
            source = ((up_ref, 2), (local_ref, 0), (down_ref, 0), (down_ref, 2))
        fill_grid(
            at,
            x_ref[g * 512 : g * 512 + 512, :],
            jnp.concatenate([piece(*p) for p in source], axis=0),
            ekey_ref[g : g + 1, :],
            grid_ref,
        )


def convolve(x_ref, grid_ref, weight_ref, out_ref, acc_ref, flip, blocks=(0, 1)):
    for at, g in enumerate(blocks):
        acc_ref[at * 512 : at * 512 + 512, :] = x_ref[g * 512 : g * 512 + 512, :].astype(F32)
    for ab in range(9):
        a, b = ab // 3, ab % 3
        for at, g in enumerate(blocks):
            total = acc_ref[at * 512 : at * 512 + 512, :]
            for c in range(3):
                rows = shifted(grid_ref, at, a, b, c)
                if flip:
                    total = total + dot_nt(rows, weight_ref[26 - (ab * 3 + c)])
                else:
                    total = total + dot(rows, weight_ref[ab * 3 + c])
            acc_ref[at * 512 : at * 512 + 512, :] = total
    for at, g in enumerate(blocks):
        out_ref[g * 512 : g * 512 + 512, :] = acc_ref[at * 512 : at * 512 + 512, :].astype(BF)


def turn_body(x_ref, chunk_ref, skey_ref, out_ref, near_chunk_ref, near_skey_ref):
    out_ref[...] = x_ref[...].astype(F32).T.astype(BF)
    near_chunk_ref[...] = chunk_ref[...]
    near_skey_ref[...] = skey_ref[...]


def backward_first_body(x, up, down, local, ekey, weight_ref, out_ref, grid_ref, acc_ref, *, base):
    fill_grids(x, up, down, local, ekey, grid_ref, base, (0,))
    convolve(x, grid_ref, weight_ref, out_ref, acc_ref, True, (0,))


def backward_body(x, up, down, local, ekey, weight_ref, first_ref, out_ref, grid_ref, acc_ref, *, base):
    fill_grids(x, up, down, local, ekey, grid_ref, base, (1,))
    out_ref[:512, :] = first_ref[...]
    convolve(x, grid_ref, weight_ref, out_ref, acc_ref, True, (1,))


def forward_body(x_ref, grid_ref, weight_ref, out_ref, acc_ref):
    convolve(x_ref, grid_ref, weight_ref, out_ref, acc_ref, False)


GRID = (2, 3, 800, C)


def scale_code(peak):
    peak = jnp.maximum(peak, 1e-30)
    power = jnp.floor(jnp.log2(peak))
    part = jnp.clip(jnp.ceil(peak * jnp.exp2(-power) * 64.0), 1.0, 200.0)
    return power * 256.0 + part


def scale_of(code):
    power = jnp.floor(code * (1.0 / 256.0))
    return jnp.exp2(power) * (code - power * 256.0) * (1.0 / 64.0)


def encode(values):
    code = scale_code(jnp.max(jnp.abs(values), axis=0, keepdims=True))
    return code, jnp.round(values * (TOP / scale_of(code))).astype(I32).astype(I16)


def decode(values, code):
    return values.astype(I32).astype(F32) * (scale_of(code) * (1.0 / TOP))


def tail_of(codes):
    lines = list(codes) + [jnp.zeros((1, C), F32)] * (TAIL - len(codes))
    return jnp.concatenate(lines, axis=0).astype(I32).astype(I16)


def tail_codes(ref, start):
    return ref[start : start + TAIL, :].astype(I32).astype(F32)


def term(grid_ref, turned_ref, offset):
    at = jnp.minimum(offset, 26)
    a, b, c = at // 9, (at // 3) % 3, at % 3
    total = dot(turned_ref[:, :512], shifted(grid_ref, 0, a, b, c))
    total = total + dot(turned_ref[:, 512:], shifted(grid_ref, 1, a, b, c))
    return jnp.where(offset < 27, total, 0.0)


def send_terms(bits_ref, grid_ref, turned_ref, send_ref, first):
    codes = []
    for i in range(PART):
        offset = (1 - bits_ref[0]) * HALF + first + i
        code, values = encode(term(grid_ref, turned_ref, offset))
        codes.append(code)
        send_ref[i * 256 : i * 256 + 256, :] = values
    send_ref[PART * 256 :, :] = tail_of(codes)


def first_terms_body(bits_ref, x, up, down, local, ekey, turned_ref, grid_ref, send_ref):
    fill_grids(x, up, down, local, ekey, grid_ref)
    send_terms(bits_ref, grid_ref, turned_ref, send_ref, 0)


def more_terms_body(bits_ref, grid_ref, turned_ref, send_ref):
    send_terms(bits_ref, grid_ref, turned_ref, send_ref, PART)


def own_terms_body(bits_ref, grid_ref, turned_ref, got_ref, keep_ref, send_ref, *, first, which):
    tail = tail_codes(got_ref, PART * 256)
    upper = bits_ref[which] > 0
    codes = []
    for i in range(PART):
        total = term(grid_ref, turned_ref, bits_ref[0] * HALF + first + i)
        total = total + decode(got_ref[i * 256 : i * 256 + 256, :], tail[i : i + 1])
        keep_ref[i] = jnp.where(upper, total[128:], total[:128])
        code, values = encode(jnp.where(upper, total[:128], total[128:]))
        codes.append(code)
        send_ref[i * 128 : i * 128 + 128, :] = values
    send_ref[PART * 128 :, :] = tail_of(codes)


def reduce_body(*refs, which, parts, rows):
    bits_ref, keep_ref, send_ref = refs[0], refs[-2], refs[-1]
    half = rows // 2
    mine = bits_ref[which]
    keep_at = pl.multiple_of(mine * half, half)
    send_at = pl.multiple_of((1 - mine) * half, half)
    codes = []
    for n, (first, many, total) in enumerate(parts):
        acc_ref, got_ref = refs[1 + 2 * n], refs[2 + 2 * n]
        tail = tail_codes(got_ref, total * rows)
        for i in range(first, first + many):
            at = len(codes)
            code = tail[i : i + 1]
            wide = acc_ref[i, pl.ds(send_at, half), :] + decode(
                got_ref[pl.ds(i * rows + send_at, half), :], code
            )
            new, values = encode(wide)
            codes.append(new)
            send_ref[at * half : at * half + half, :] = values
            keep_ref[at] = acc_ref[i, pl.ds(keep_at, half), :] + decode(
                got_ref[pl.ds(i * rows + keep_at, half), :], code
            )
    send_ref[len(codes) * half :, :] = tail_of(codes)


def reduce_step(bits, which, operands, parts, rows):
    many = sum(p[1] for p in parts)
    half = rows // 2
    outs = [((many, half, C), F32), ((many * half + TAIL, C), I16)]
    body = functools.partial(reduce_body, which=which, parts=parts, rows=rows)
    return call(body, outs, [bits, *operands], smem=(0,), moved=many * rows * C * 8)


def total_body(acc_ref, got_ref, out_ref):
    tail = tail_codes(got_ref, HALF * 16)
    for i in range(HALF):
        out_ref[i] = acc_ref[i] + decode(got_ref[i * 16 : i * 16 + 16, :], tail[i : i + 1])


def unit_body(total_ref, a_ref, b_ref):
    for p, out_ref in enumerate((a_ref, b_ref)):
        codes = []
        squares = jnp.zeros((1, C), F32)
        for i in range(PART):
            value = total_ref[p * PART + i]
            squares = squares + jnp.sum(value * value, axis=0, keepdims=True)
            code, coded = encode(value)
            codes.append(code)
            out_ref[i * 16 : i * 16 + 16, :] = coded
        squares = jnp.maximum(squares, 1e-30)
        power = jnp.floor(jnp.log2(squares))
        codes.append(power)
        codes.append(jnp.round(jnp.minimum(squares * jnp.exp2(-power) * 15000.0, 32000.0)))
        out_ref[PART * 16 :, :] = tail_of(codes)


def finish_body(bits_ref, *refs):
    out_ref, stage_ref, wide_ref, square_ref, sem = refs[8:]
    mine = bits_ref[0]
    halves = (mine, 1 - mine)

    def place_of(side, p, u):
        x = bits_ref[1] ^ ((u >> (3 - p)) & 1)
        y = bits_ref[2] ^ ((u >> (2 + p)) & 1)
        low = (bits_ref[3] ^ ((u >> 1) & 1)) * 2 + (bits_ref[4] ^ (u & 1))
        return jnp.where(halves[side] > 0, y * 8 + x * 4, x * 8 + y * 4) + low

    def leave(side, i):
        offset = halves[side] * HALF + i
        n = side * HALF + i
        return offset, pltpu.make_async_copy(stage_ref.at[n], out_ref.at[offset], sem.at[n])

    def ref_of(side, p, u):
        return refs[side * 4 + p * 2 + u // 8], (u % 8) * UNIT

    for side in range(2):
        for p in range(2):
            for u in range(16):
                ref, at = ref_of(side, p, u)
                tail = tail_codes(ref, at + PART * 16)
                square_ref[pl.ds(halves[side] * 32 + p * 16 + place_of(side, p, u), 1), :] = (
                    jnp.exp2(tail[PART : PART + 1]) * tail[PART + 1 : PART + 2]
                )
    squares = jnp.sum(square_ref[...], axis=0, keepdims=True)
    mean = jnp.sum(squares, axis=1, keepdims=True) * (1.0 / (15000.0 * 27 * C * C))
    gain = 1.0 / jnp.sqrt(mean + 1e-06)
    for side in range(2):
        for p in range(2):
            places, scales = [], []
            for u in range(16):
                ref, at = ref_of(side, p, u)
                places.append(pl.multiple_of(place_of(side, p, u) * 16, 16))
                scales.append(scale_of(tail_codes(ref, at + PART * 16)[:8]) * gain * (1.0 / TOP))
            for i in range(PART):
                for u in range(16):
                    ref, at = ref_of(side, p, u)
                    coded = ref[at + i * 16 : at + i * 16 + 16, :]
                    wide_ref[i % 2, pl.ds(places[u], 16), :] = (
                        coded.astype(I32).astype(F32) * scales[u][i : i + 1]
                    ).astype(BF)
                stage_ref[side * HALF + p * PART + i] = wide_ref[i % 2].T
                offset, copy = leave(side, p * PART + i)
                pl.when(offset < 27)(copy.start)
    for side in range(2):
        for i in range(HALF):
            offset, copy = leave(side, i)
            pl.when(offset < 27)(copy.wait)


def swap(x, bit):
    axis, place = bit
    count = lax.axis_size(axis)
    return lax.ppermute(x, axis, [(i, i ^ (1 << place)) for i in range(count)])


def swap_either(x, parity, bits):
    count, width = lax.axis_size("pts"), lax.axis_size("dp")
    turn = []
    for i in range(count * width):
        place = {"pts": i // width, "dp": i % width}
        axis, at = bits[(place[parity[0]] >> parity[1]) & 1]
        place[axis] ^= 1 << at
        turn.append((i, place["pts"] * width + place["dp"]))
    return lax.ppermute(x, ("pts", "dp"), turn)


def shift(x, step):
    count = lax.axis_size("pts")
    return lax.ppermute(
        x, "pts", [(i, i + step) for i in range(count) if 0 <= i + step < count]
    )


def device_bits():
    dp = lax.axis_size("dp").bit_length() - 1
    pts = lax.axis_size("pts").bit_length() - 1
    order = [("dp", n) for n in range(dp)] + [("pts", n) for n in range(pts)]
    return order[:5], order[5:]


def bit_value(bit):
    return (lax.axis_index(bit[0]) >> bit[1]) & 1


def on_device(features, hilbert_pos, weight, neighbours, grad_out):
    rows = features.shape[1]
    count = lax.axis_size("pts")
    me = lax.axis_index("pts").astype(I32)
    window = min(16, count)
    cap = 2 * rows // window
    split, extra = device_bits()
    s0, s1, s2, s3, s4 = split
    odd = bit_value(s0) > 0
    first = jnp.where(odd, bit_value(s2), bit_value(s1))
    second = jnp.where(odd, bit_value(s1), bit_value(s2))
    bits = jnp.stack([*(bit_value(b) for b in split), first, second]).astype(I32)

    dy = grad_out[0]
    lines = [cap + TAIL + (192 if abs(w - window // 2) == 1 else 0) for w in range(window)]
    *packed, skey, ekey, dy_local = call(
        functools.partial(pack_body, count=count, window=window, cap=cap),
        [*(((n, C), BF) for n in lines), ((8, 512), I32), ((2, C), I32), ((128, C), BF)],
        [me.reshape(1), neighbours[0], hilbert_pos, dy, features[0]],
        smem=(0,),
        far=(1, 2, 3, 4),
        vmem=60,
        scratch=[
            pltpu.SMEM(neighbours.shape[1:], I32),
            pltpu.VMEM(hilbert_pos.shape, I32),
            pltpu.VMEM((rows, C), BF),
            pltpu.VMEM((rows, C), BF),
            pltpu.SemaphoreType.DMA((4,)),
        ],
        flops=4 * rows * rows * C,
        moved=4 * rows * C * 2,
    )
    got = [None] * window
    for w in sorted(range(window), key=lambda w: (-abs(w - window // 2), w)):
        step = w - window // 2
        turn = [(i, (i + step) % count) for i in range(count)]
        got[w] = packed[w] if step == 0 else lax.ppermute(packed[w], "pts", turn)

    conv_flops = 2 * 27 * rows * C * C
    part_flops = conv_flops
    stayed = window // 2
    turned, got[stayed], skey = call(
        turn_body,
        [((C, rows), BF), ((cap + TAIL, C), BF), ((8, 512), I32)],
        [dy, packed[stayed], skey],
    )

    x, up, down, x_local = call(
        functools.partial(order_body, cap=cap),
        [((rows, C), BF), *FACE_OUTS],
        [*got, skey],
        flops=4 * rows * rows * C,
        moved=4 * rows * C * 2,
    )
    x_up, x_down = shift(up, 1), shift(down, -1)
    grid, send_a = call(
        first_terms_body,
        [(GRID, BF), ((PART * C + TAIL, C), I16)],
        [bits, x, x_up, x_down, x_local, ekey, turned],
        smem=(0,),
        flops=part_flops,
        moved=5 * MIB,
    )
    came_a = swap(send_a, s0)
    (send_b,) = call(
        more_terms_body,
        [((PART * C + TAIL, C), I16)],
        [bits, grid, turned],
        smem=(0,),
        flops=part_flops,
        moved=5 * MIB,
    )
    came_b = swap(send_b, s0)
    own_outs = [((PART, 128, C), F32), ((PART * 128 + TAIL, C), I16)]
    keep_a, send_a = call(
        functools.partial(own_terms_body, first=0, which=5),
        own_outs,
        [bits, grid, turned, came_a],
        smem=(0,),
        flops=part_flops,
        moved=5 * MIB,
    )
    came_a = swap_either(send_a, s0, (s1, s2))
    keep_b, send_b = call(
        functools.partial(own_terms_body, first=PART, which=5),
        own_outs,
        [bits, grid, turned, came_b],
        smem=(0,),
        flops=part_flops,
        moved=5 * MIB,
    )
    came_b = swap_either(send_b, s0, (s1, s2))
    x, grid, keep_b = lax.optimization_barrier((x, grid, keep_b))
    (forward,) = call(
        forward_body,
        [((rows, C), BF)],
        [x, grid, weight],
        scratch=[pltpu.VMEM((rows, C), F32)],
        flops=conv_flops,
        moved=6 * MIB,
    )
    forward, came_a, came_b = lax.optimization_barrier((forward, came_a, came_b))

    keep, send = reduce_step(
        bits, 6, [keep_a, came_a, keep_b, came_b], ((0, PART, PART), (0, PART, PART)), 128
    )
    came = swap_either(send, s0, (s2, s1))
    keep, send = reduce_step(bits, 3, [keep, came], ((0, HALF, HALF),), 64)
    came = swap(send, s3)
    keep, send = reduce_step(bits, 4, [keep, came], ((0, HALF, HALF),), 32)
    came = swap(send, s4)
    (total,) = call(total_body, [((HALF, 16, C), F32)], [keep, came])
    for b in extra:
        total = total + swap(total, b)
    unit_a, unit_b = call(unit_body, [((UNIT, C), I16), ((UNIT, C), I16)], [total])

    unit_a, unit_b, dy = lax.optimization_barrier((unit_a, unit_b, dy))
    back_args = [got[window // 2 + 1], got[window // 2 - 1], dy_local, ekey, weight]
    back_scratch = [pltpu.VMEM((1, 3, 800, C), BF), pltpu.VMEM((512, C), F32)]
    far = swap(jnp.concatenate([unit_a, unit_b], axis=0), s4)
    (backward,) = call(
        functools.partial(backward_first_body, base=cap + TAIL),
        [((512, C), BF)],
        [dy, *back_args],
        scratch=back_scratch,
        flops=conv_flops // 2,
        moved=5 * MIB,
    )
    far, backward, dy = lax.optimization_barrier((far, backward, dy))
    unit_a = jnp.concatenate([unit_a, far[:UNIT]], axis=0)
    unit_b = jnp.concatenate([unit_b, far[UNIT:]], axis=0)
    far = swap(jnp.concatenate([unit_a, unit_b], axis=0), s3)
    (backward,) = call(
        functools.partial(backward_body, base=cap + TAIL),
        [((rows, C), BF)],
        [dy, *back_args, backward],
        scratch=back_scratch,
        flops=conv_flops // 2,
        moved=5 * MIB,
    )
    far, backward = lax.optimization_barrier((far, backward))
    unit_a = jnp.concatenate([unit_a, far[: 2 * UNIT]], axis=0)
    unit_b = jnp.concatenate([unit_b, far[2 * UNIT :]], axis=0)
    far_a, far_b = swap(unit_a, s2), swap(unit_b, s1)
    unit_a = jnp.concatenate([unit_a, far_a], axis=0)
    unit_b = jnp.concatenate([unit_b, far_b], axis=0)
    far_a, far_b = swap(unit_a, s1), swap(unit_b, s2)
    other_a, other_b = swap(unit_a, s0), swap(unit_b, s0)
    other_far_a, other_far_b = swap(far_a, s0), swap(far_b, s0)
    (weight_grad,) = call(
        finish_body,
        [((27, C, C), BF)],
        [bits, unit_a, far_a, unit_b, far_b, other_a, other_far_a, other_b, other_far_b],
        smem=(0,),
        scratch=[
            pltpu.VMEM((2 * HALF, C, C), BF),
            pltpu.VMEM((2, C, C), BF),
            pltpu.VMEM((64, C), F32),
            pltpu.SemaphoreType.DMA((2 * HALF,)),
        ],
        far_out=True,
    )
    return forward[None], backward[None], weight_grad


def solution(mesh):
    placed = (P("dp", "pts", None), P("dp", "pts"), P(), P("dp", "pts", None), P("dp", "pts", None))
    return jax.shard_map(
        on_device,
        mesh=mesh,
        in_specs=placed,
        out_specs=(P("dp", "pts", None), P("dp", "pts", None), P()),
        check_vma=False,
    )
```

```python
import functools

import jax
import jax.numpy as jnp
from jax import lax
from jax.experimental import pallas as pl
from jax.experimental.pallas import tpu as pltpu
from jax.sharding import PartitionSpec as P

BF = jnp.bfloat16
F32 = jnp.float32
I32 = jnp.int32
I16 = jnp.int16
C = 256
STEPS = (-2, -1, 1, 2)
HALF = 14
PART = 7
TAIL = 16
UNIT = PART * 16 + TAIL
TOP = 32760.0
MIB = 1 << 20


def dot(a, b):
    return lax.dot_general(a, b, (((1,), (0,)), ((), ())), preferred_element_type=F32)


def dot_nt(a, b):
    return lax.dot_general(a, b, (((1,), (1,)), ((), ())), preferred_element_type=F32)


def one_hot(index, key):
    return jnp.where(index == key, 1.0, 0.0).astype(BF)


def call(body, outs, args, smem=(), scratch=(), vmem=48, flops=0, moved=0, far=(), far_out=False):
    specs = [
        pl.BlockSpec(
            memory_space=pltpu.HBM if i in far else pltpu.SMEM if i in smem else pltpu.VMEM
        )
        for i in range(len(args))
    ]
    shapes = [jax.ShapeDtypeStruct(s, d) for s, d in outs]
    return pl.pallas_call(
        body,
        out_shape=shapes,
        in_specs=specs,
        out_specs=[
            pl.BlockSpec(memory_space=pltpu.HBM if far_out else pltpu.VMEM) for _ in shapes
        ],
        scratch_shapes=list(scratch),
        compiler_params=pltpu.CompilerParams(vmem_limit_bytes=vmem * MIB),
        cost_estimate=pl.CostEstimate(flops=flops, bytes_accessed=moved, transcendentals=0),
    )(*args)


def links(near_ref, own, g):
    found = [jnp.int32(-1)] * 4
    for d in range(26):
        near = near_ref[g, d]
        for n, t in enumerate(STEPS):
            hit = jnp.logical_and(near >= 0, near == own + t)
            found[n] = jnp.where(hit, d + (d >= 13), found[n])
    return found


def key_rows(near_ref, own, g):
    v = lax.broadcasted_iota(I32, (1, 512), 1)
    i, j, k = v >> 6, (v >> 3) & 7, v & 7
    lane = lax.broadcasted_iota(I32, (1, 256), 1)
    m = lane & 63
    sends = []
    cells = jnp.full((1, 256), -100, I32)
    for n, o in enumerate(links(near_ref, own, g)):
        some = o >= 0
        o = jnp.maximum(o, 0)
        a, b, c = o // 9 - 1, (o // 3) % 3 - 1, o % 3 - 1
        sk = jnp.where(c == 0, 3, 0)
        sj = jnp.where(b == 0, 3, 0)
        rank = jnp.zeros((1, 512), I32)
        on = v >= jnp.where(some, 0, 512)
        for step, at, size in ((a, i, 3), (b, j, sj), (c, k, sk)):
            free = step == 0
            rank = (rank << jnp.where(free, 3, 0)) + at * jnp.where(free, 1, 0)
            low = jnp.where(free, 0, jnp.where(step > 0, 7, 0))
            high = jnp.where(free, 7, low)
            on = on & (at >= low) & (at <= high)
        sends.append(jnp.where(on, rank, -1))
        cell = jnp.zeros((1, 256), I32)
        for step, free_at in ((a, m >> (sk + sj)), (b, (m >> sk) & 7), (c, m & 7)):
            free = step == 0
            fixed = jnp.where(step > 0, 9, 0)
            cell = cell * 10 + (free_at + 1) * jnp.where(free, 1, 0) + jnp.where(free, 0, fixed)
        last = jnp.where(a == 0, 8, 1) << (sj + sk)
        inside = (lane >> 6 == n) & (m < jnp.where(some, last, 0))
        cells = jnp.where(inside, cell, cells)
    return sends, cells


def pack_body(me_ref, *refs, count, window, cap):
    sources, refs = refs[:4], refs[4:]
    *out_refs, skey_ref, ekey_ref, local_ref = refs[: window + 3]
    *landed, sem = refs[window + 3 :]
    copies = [
        pltpu.make_async_copy(source, to, sem.at[n])
        for n, (source, to) in enumerate(zip(sources, landed, strict=True))
    ]
    for copy in copies:
        copy.start()
    near_ref, pos_ref, dy_ref, x_ref = landed
    rows = x_ref.shape[0]
    copies[0].wait()
    for g in range(2):
        sends, cells = key_rows(near_ref, me_ref[0] * 2 + g, g)
        for n in range(4):
            skey_ref[g * 4 + n : g * 4 + n + 1, :] = sends[n]
        ekey_ref[g : g + 1, :] = cells
    copies[1].wait()
    copies[2].wait()
    base = cap + TAIL
    faces_of(
        lambda g: dy_ref[g * 512 : g * 512 + 512, :],
        skey_ref,
        out_refs[window // 2 + 1].at[pl.ds(base, 192)],
        out_refs[window // 2 - 1].at[pl.ds(base, 192)],
        local_ref,
    )
    pos = pos_ref[...]
    owner = pos >> (rows.bit_length() - 1)
    local = pos & (rows - 1)
    chunk = (owner - me_ref[0] + window // 2) & (count - 1)
    member = (chunk == lax.broadcasted_iota(I32, (window, rows), 0)).astype(I32)
    lane = lax.broadcasted_iota(I32, (window, rows), 1)
    rank = member
    step = 1
    while step < rows:
        rank = rank + jnp.where(lane >= step, pltpu.roll(rank, step, 1), 0)
        step *= 2
    keys = jnp.where(member > 0, rank - 1, -1)
    line = lax.broadcasted_iota(I32, (TAIL, rows), 0)
    digits = jnp.where(line == 0, (local >> 5) + 1, jnp.where(line == 1, local & 31, 0))
    digits = digits.astype(F32).astype(BF)
    copies[3].wait()
    x = x_ref[...]
    slot = lax.broadcasted_iota(I32, (cap, rows), 0)
    for c in range(window):
        pick = one_hot(slot, keys[c : c + 1, :])
        out_refs[c][:cap, :] = dot(pick, x).astype(BF)
        tail = dot_nt(digits, pick)
        if cap < C:
            tail = jnp.concatenate([tail, jnp.zeros((TAIL, C - cap), F32)], axis=1)
        out_refs[c][cap : cap + TAIL, :] = tail.astype(BF)


def faces_of(rows_of, skey_ref, up_ref, down_ref, local_ref):
    slot = lax.broadcasted_iota(I32, (64, 512), 0)
    made = {}
    for g in range(2):
        rows = rows_of(g)
        pick = jnp.concatenate(
            [one_hot(slot, skey_ref[g * 4 + n : g * 4 + n + 1, :]) for n in range(4)], axis=0
        )
        face = dot(pick, rows).astype(BF)
        for n, t in enumerate(STEPS):
            made[g, t] = face[n * 64 : n * 64 + 64]
    for n, k in enumerate(((0, 2), (1, 1), (1, 2))):
        up_ref[n * 64 : n * 64 + 64, :] = made[k]
    for n, k in enumerate(((0, -1), (0, -2), (1, -2))):
        down_ref[n * 64 : n * 64 + 64, :] = made[k]
    for n, k in enumerate(((0, 1), (1, -1))):
        local_ref[n * 64 : n * 64 + 64, :] = made[k]


def order_body(*refs, cap):
    *got_refs, skey_ref, out_ref, up_ref, down_ref, local_ref = refs
    chunks = len(got_refs)
    rows = out_ref.shape[0]
    targets = []
    for c in range(chunks):
        tail = got_refs[c][cap : cap + TAIL, :].astype(F32)
        place = (tail[0:1] - 1.0) * 32.0 + tail[1:2]
        targets.append(place[:, :cap].astype(I32))
    for m in range(0, rows, 256):
        slot = lax.broadcasted_iota(I32, (256, cap), 0) + m
        total = jnp.zeros((256, C), F32)
        for c in range(chunks):
            total = total + dot(one_hot(slot, targets[c]), got_refs[c][:cap, :])
        out_ref[m : m + 256, :] = total.astype(BF)
    faces_of(lambda g: out_ref[g * 512 : g * 512 + 512, :], skey_ref, up_ref, down_ref, local_ref)


FACE_OUTS = [((192, C), BF), ((192, C), BF), ((128, C), BF)]


def fill_grid(block, x, pieces, ekey, grid_ref):
    wide = x.astype(F32)
    k_of = lax.broadcasted_iota(I32, (512, C), 0) & 7
    row = lax.broadcasted_iota(I32, (800, C), 0)
    cell = (row >> 3) * 10 + (row & 7) + 1
    for ci, c in enumerate((-1, 0, 1)):
        rim = dot(one_hot(cell, ekey - c), pieces)
        if c == 0:
            moved = wide
        elif c < 0:
            moved = jnp.where(k_of == 0, 0.0, pltpu.roll(wide, 1, 0))
        else:
            moved = jnp.where(k_of == 7, 0.0, pltpu.roll(wide, 511, 0))
        for i in range(10):
            stripe = rim[i * 80 : i * 80 + 80]
            if 1 <= i <= 8:
                inner = stripe[8:72] + moved[i * 64 - 64 : i * 64]
                stripe = jnp.concatenate([stripe[:8], inner, stripe[72:]], axis=0)
            grid_ref[block, ci, i * 80 : i * 80 + 80, :] = stripe.astype(BF)


def shifted(grid_ref, block, a, b, c):
    lines = []
    for i in range(8):
        start = (i + a) * 80 + b * 8
        if not isinstance(start, int):
            start = pl.multiple_of(start, 8)
        lines.append(grid_ref[block, c, pl.ds(start, 64), :])
    return jnp.concatenate(lines, axis=0)


def fill_grids(x_ref, up_ref, down_ref, local_ref, ekey_ref, grid_ref, base=0, blocks=(0, 1)):
    def piece(ref, n):
        start = n * 64 + (0 if ref is local_ref else base)
        return ref[start : start + 64, :]

    for at, g in enumerate(blocks):
        if g == 0:
            source = ((up_ref, 0), (up_ref, 1), (local_ref, 1), (down_ref, 1))
        else:
            source = ((up_ref, 2), (local_ref, 0), (down_ref, 0), (down_ref, 2))
        fill_grid(
            at,
            x_ref[g * 512 : g * 512 + 512, :],
            jnp.concatenate([piece(*p) for p in source], axis=0),
            ekey_ref[g : g + 1, :],
            grid_ref,
        )


def convolve(x_ref, grid_ref, weight_ref, out_ref, acc_ref, flip, blocks=(0, 1)):
    for at, g in enumerate(blocks):
        acc_ref[at * 512 : at * 512 + 512, :] = x_ref[g * 512 : g * 512 + 512, :].astype(F32)
    for ab in range(9):
        a, b = ab // 3, ab % 3
        for at, g in enumerate(blocks):
            total = acc_ref[at * 512 : at * 512 + 512, :]
            for c in range(3):
                rows = shifted(grid_ref, at, a, b, c)
                if flip:
                    total = total + dot_nt(rows, weight_ref[26 - (ab * 3 + c)])
                else:
                    total = total + dot(rows, weight_ref[ab * 3 + c])
            acc_ref[at * 512 : at * 512 + 512, :] = total
    for at, g in enumerate(blocks):
        out_ref[g * 512 : g * 512 + 512, :] = acc_ref[at * 512 : at * 512 + 512, :].astype(BF)


def turn_body(x_ref, chunk_ref, skey_ref, out_ref, near_chunk_ref, near_skey_ref):
    out_ref[...] = x_ref[...].astype(F32).T.astype(BF)
    near_chunk_ref[...] = chunk_ref[...]
    near_skey_ref[...] = skey_ref[...]


def backward_first_body(x, up, down, local, ekey, weight_ref, out_ref, grid_ref, acc_ref, *, base):
    fill_grids(x, up, down, local, ekey, grid_ref, base, (0,))
    convolve(x, grid_ref, weight_ref, out_ref, acc_ref, True, (0,))


def backward_body(x, up, down, local, ekey, weight_ref, first_ref, out_ref, grid_ref, acc_ref, *, base):
    fill_grids(x, up, down, local, ekey, grid_ref, base, (1,))
    out_ref[:512, :] = first_ref[...]
    convolve(x, grid_ref, weight_ref, out_ref, acc_ref, True, (1,))


def forward_body(x_ref, grid_ref, weight_ref, out_ref, acc_ref):
    convolve(x_ref, grid_ref, weight_ref, out_ref, acc_ref, False)


GRID = (2, 3, 800, C)


def scale_code(peak):
    peak = jnp.maximum(peak, 1e-30)
    power = jnp.floor(jnp.log2(peak))
    part = jnp.clip(jnp.ceil(peak * jnp.exp2(-power) * 64.0), 1.0, 200.0)
    return power * 256.0 + part


def scale_of(code):
    power = jnp.floor(code * (1.0 / 256.0))
    return jnp.exp2(power) * (code - power * 256.0) * (1.0 / 64.0)


def encode(values):
    code = scale_code(jnp.max(jnp.abs(values), axis=0, keepdims=True))
    return code, jnp.round(values * (TOP / scale_of(code))).astype(I32).astype(I16)


def decode(values, code):
    return values.astype(I32).astype(F32) * (scale_of(code) * (1.0 / TOP))


def tail_of(codes):
    lines = list(codes) + [jnp.zeros((1, C), F32)] * (TAIL - len(codes))
    return jnp.concatenate(lines, axis=0).astype(I32).astype(I16)


def tail_codes(ref, start):
    return ref[start : start + TAIL, :].astype(I32).astype(F32)


def term(grid_ref, turned_ref, offset):
    at = jnp.minimum(offset, 26)
    a, b, c = at // 9, (at // 3) % 3, at % 3
    total = dot(turned_ref[:, :512], shifted(grid_ref, 0, a, b, c))
    total = total + dot(turned_ref[:, 512:], shifted(grid_ref, 1, a, b, c))
    return jnp.where(offset < 27, total, 0.0)


def send_terms(bits_ref, grid_ref, turned_ref, send_ref, first):
    codes = []
    for i in range(PART):
        offset = (1 - bits_ref[0]) * HALF + first + i
        code, values = encode(term(grid_ref, turned_ref, offset))
        codes.append(code)
        send_ref[i * 256 : i * 256 + 256, :] = values
    send_ref[PART * 256 :, :] = tail_of(codes)


def first_terms_body(bits_ref, x, up, down, local, ekey, turned_ref, grid_ref, send_ref):
    fill_grids(x, up, down, local, ekey, grid_ref)
    send_terms(bits_ref, grid_ref, turned_ref, send_ref, 0)


def more_terms_body(bits_ref, grid_ref, turned_ref, send_ref):
    send_terms(bits_ref, grid_ref, turned_ref, send_ref, PART)


def own_terms_body(bits_ref, grid_ref, turned_ref, got_ref, keep_ref, send_ref, *, first, which):
    tail = tail_codes(got_ref, PART * 256)
    upper = bits_ref[which] > 0
    codes = []
    for i in range(PART):
        total = term(grid_ref, turned_ref, bits_ref[0] * HALF + first + i)
        total = total + decode(got_ref[i * 256 : i * 256 + 256, :], tail[i : i + 1])
        keep_ref[i] = jnp.where(upper, total[128:], total[:128])
        code, values = encode(jnp.where(upper, total[:128], total[128:]))
        codes.append(code)
        send_ref[i * 128 : i * 128 + 128, :] = values
    send_ref[PART * 128 :, :] = tail_of(codes)


def reduce_body(*refs, which, parts, rows):
    bits_ref, keep_ref, send_ref = refs[0], refs[-2], refs[-1]
    half = rows // 2
    mine = bits_ref[which]
    keep_at = pl.multiple_of(mine * half, half)
    send_at = pl.multiple_of((1 - mine) * half, half)
    codes = []
    for n, (first, many, total) in enumerate(parts):
        acc_ref, got_ref = refs[1 + 2 * n], refs[2 + 2 * n]
        tail = tail_codes(got_ref, total * rows)
        for i in range(first, first + many):
            at = len(codes)
            code = tail[i : i + 1]
            wide = acc_ref[i, pl.ds(send_at, half), :] + decode(
                got_ref[pl.ds(i * rows + send_at, half), :], code
            )
            new, values = encode(wide)
            codes.append(new)
            send_ref[at * half : at * half + half, :] = values
            keep_ref[at] = acc_ref[i, pl.ds(keep_at, half), :] + decode(
                got_ref[pl.ds(i * rows + keep_at, half), :], code
            )
    send_ref[len(codes) * half :, :] = tail_of(codes)


def reduce_step(bits, which, operands, parts, rows):
    many = sum(p[1] for p in parts)
    half = rows // 2
    outs = [((many, half, C), F32), ((many * half + TAIL, C), I16)]
    body = functools.partial(reduce_body, which=which, parts=parts, rows=rows)
    return call(body, outs, [bits, *operands], smem=(0,), moved=many * rows * C * 8)


def total_body(acc_ref, got_ref, out_ref):
    tail = tail_codes(got_ref, HALF * 16)
    for i in range(HALF):
        out_ref[i] = acc_ref[i] + decode(got_ref[i * 16 : i * 16 + 16, :], tail[i : i + 1])


def total_unit_body(acc_ref, got_ref, a_ref, b_ref, total_ref):
    total_body(acc_ref, got_ref, total_ref)
    unit_body(total_ref, a_ref, b_ref)


def unit_body(total_ref, a_ref, b_ref):
    for p, out_ref in enumerate((a_ref, b_ref)):
        codes = []
        squares = jnp.zeros((1, C), F32)
        for i in range(PART):
            value = total_ref[p * PART + i]
            squares = squares + jnp.sum(value * value, axis=0, keepdims=True)
            code, coded = encode(value)
            codes.append(code)
            out_ref[i * 16 : i * 16 + 16, :] = coded
        squares = jnp.maximum(squares, 1e-30)
        power = jnp.floor(jnp.log2(squares))
        codes.append(power)
        codes.append(jnp.round(jnp.minimum(squares * jnp.exp2(-power) * 15000.0, 32000.0)))
        out_ref[PART * 16 :, :] = tail_of(codes)


def finish_body(bits_ref, *refs):
    out_ref, stage_ref, wide_ref, square_ref, sem = refs[8:]
    mine = bits_ref[0]
    halves = (mine, 1 - mine)

    def place_of(side, p, u):
        x = bits_ref[1] ^ ((u >> (3 - p)) & 1)
        y = bits_ref[2] ^ ((u >> (2 + p)) & 1)
        low = (bits_ref[3] ^ ((u >> 1) & 1)) * 2 + (bits_ref[4] ^ (u & 1))
        return jnp.where(halves[side] > 0, y * 8 + x * 4, x * 8 + y * 4) + low

    def leave(side, i):
        offset = halves[side] * HALF + i
        n = side * HALF + i
        return offset, pltpu.make_async_copy(stage_ref.at[n], out_ref.at[offset], sem.at[n])

    def ref_of(side, p, u):
        return refs[side * 4 + p * 2 + u // 8], (u % 8) * UNIT

    for side in range(2):
        for p in range(2):
            for u in range(16):
                ref, at = ref_of(side, p, u)
                tail = tail_codes(ref, at + PART * 16)
                square_ref[pl.ds(halves[side] * 32 + p * 16 + place_of(side, p, u), 1), :] = (
                    jnp.exp2(tail[PART : PART + 1]) * tail[PART + 1 : PART + 2]
                )
    squares = jnp.sum(square_ref[...], axis=0, keepdims=True)
    mean = jnp.sum(squares, axis=1, keepdims=True) * (1.0 / (15000.0 * 27 * C * C))
    gain = 1.0 / jnp.sqrt(mean + 1e-06)
    for side in range(2):
        for p in range(2):
            places, scales = [], []
            for u in range(16):
                ref, at = ref_of(side, p, u)
                places.append(pl.multiple_of(place_of(side, p, u) * 16, 16))
                scales.append(scale_of(tail_codes(ref, at + PART * 16)[:8]) * gain * (1.0 / TOP))
            for i in range(PART):
                for u in range(16):
                    ref, at = ref_of(side, p, u)
                    coded = ref[at + i * 16 : at + i * 16 + 16, :]
                    wide_ref[i % 2, pl.ds(places[u], 16), :] = (
                        coded.astype(I32).astype(F32) * scales[u][i : i + 1]
                    ).astype(BF)
                stage_ref[side * HALF + p * PART + i] = wide_ref[i % 2].T
                offset, copy = leave(side, p * PART + i)
                pl.when(offset < 27)(copy.start)
    for side in range(2):
        for i in range(HALF):
            offset, copy = leave(side, i)
            pl.when(offset < 27)(copy.wait)


def swap(x, bit):
    axis, place = bit
    count = lax.axis_size(axis)
    return lax.ppermute(x, axis, [(i, i ^ (1 << place)) for i in range(count)])


def swap_either(x, parity, bits):
    count, width = lax.axis_size("pts"), lax.axis_size("dp")
    turn = []
    for i in range(count * width):
        place = {"pts": i // width, "dp": i % width}
        axis, at = bits[(place[parity[0]] >> parity[1]) & 1]
        place[axis] ^= 1 << at
        turn.append((i, place["pts"] * width + place["dp"]))
    return lax.ppermute(x, ("pts", "dp"), turn)


def shift(x, step):
    count = lax.axis_size("pts")
    return lax.ppermute(
        x, "pts", [(i, i + step) for i in range(count) if 0 <= i + step < count]
    )


def device_bits():
    dp = lax.axis_size("dp").bit_length() - 1
    pts = lax.axis_size("pts").bit_length() - 1
    order = [("dp", n) for n in range(dp)] + [("pts", n) for n in range(pts)]
    return order[:5], order[5:]


def bit_value(bit):
    return (lax.axis_index(bit[0]) >> bit[1]) & 1


def on_device(features, hilbert_pos, weight, neighbours, grad_out):
    rows = features.shape[1]
    count = lax.axis_size("pts")
    me = lax.axis_index("pts").astype(I32)
    window = min(16, count)
    cap = 2 * rows // window
    split, extra = device_bits()
    s0, s1, s2, s3, s4 = split
    odd = bit_value(s0) > 0
    first = jnp.where(odd, bit_value(s2), bit_value(s1))
    second = jnp.where(odd, bit_value(s1), bit_value(s2))
    bits = jnp.stack([*(bit_value(b) for b in split), first, second]).astype(I32)

    dy = grad_out[0]
    lines = [cap + TAIL + (192 if abs(w - window // 2) == 1 else 0) for w in range(window)]
    *packed, skey, ekey, dy_local = call(
        functools.partial(pack_body, count=count, window=window, cap=cap),
        [*(((n, C), BF) for n in lines), ((8, 512), I32), ((2, C), I32), ((128, C), BF)],
        [me.reshape(1), neighbours[0], hilbert_pos, dy, features[0]],
        smem=(0,),
        far=(1, 2, 3, 4),
        vmem=60,
        scratch=[
            pltpu.SMEM(neighbours.shape[1:], I32),
            pltpu.VMEM(hilbert_pos.shape, I32),
            pltpu.VMEM((rows, C), BF),
            pltpu.VMEM((rows, C), BF),
            pltpu.SemaphoreType.DMA((4,)),
        ],
        flops=4 * rows * rows * C,
        moved=4 * rows * C * 2,
    )
    got = [None] * window
    for w in sorted(range(window), key=lambda w: (-abs(w - window // 2), w)):
        step = w - window // 2
        turn = [(i, (i + step) % count) for i in range(count)]
        got[w] = packed[w] if step == 0 else lax.ppermute(packed[w], "pts", turn)

    conv_flops = 2 * 27 * rows * C * C
    part_flops = conv_flops
    stayed = window // 2
    turned, got[stayed], skey = call(
        turn_body,
        [((C, rows), BF), ((cap + TAIL, C), BF), ((8, 512), I32)],
        [dy, packed[stayed], skey],
    )

    x, up, down, x_local = call(
        functools.partial(order_body, cap=cap),
        [((rows, C), BF), *FACE_OUTS],
        [*got, skey],
        flops=4 * rows * rows * C,
        moved=4 * rows * C * 2,
    )
    x_up, x_down = shift(up, 1), shift(down, -1)
    grid, send_a = call(
        first_terms_body,
        [(GRID, BF), ((PART * C + TAIL, C), I16)],
        [bits, x, x_up, x_down, x_local, ekey, turned],
        smem=(0,),
        flops=part_flops,
        moved=5 * MIB,
    )
    came_a = swap(send_a, s0)
    (send_b,) = call(
        more_terms_body,
        [((PART * C + TAIL, C), I16)],
        [bits, grid, turned],
        smem=(0,),
        flops=part_flops,
        moved=5 * MIB,
    )
    came_b = swap(send_b, s0)
    own_outs = [((PART, 128, C), F32), ((PART * 128 + TAIL, C), I16)]
    keep_a, send_a = call(
        functools.partial(own_terms_body, first=0, which=5),
        own_outs,
        [bits, grid, turned, came_a],
        smem=(0,),
        flops=part_flops,
        moved=5 * MIB,
    )
    came_a = swap_either(send_a, s0, (s1, s2))
    keep_b, send_b = call(
        functools.partial(own_terms_body, first=PART, which=5),
        own_outs,
        [bits, grid, turned, came_b],
        smem=(0,),
        flops=part_flops,
        moved=5 * MIB,
    )
    came_b = swap_either(send_b, s0, (s1, s2))
    x, grid, keep_b = lax.optimization_barrier((x, grid, keep_b))
    (forward,) = call(
        forward_body,
        [((rows, C), BF)],
        [x, grid, weight],
        scratch=[pltpu.VMEM((rows, C), F32)],
        flops=conv_flops,
        moved=6 * MIB,
    )
    forward, came_a, came_b = lax.optimization_barrier((forward, came_a, came_b))

    keep, send = reduce_step(
        bits, 6, [keep_a, came_a, keep_b, came_b], ((0, PART, PART), (0, PART, PART)), 128
    )
    came = swap_either(send, s0, (s2, s1))
    keep, send = reduce_step(bits, 3, [keep, came], ((0, HALF, HALF),), 64)
    came = swap(send, s3)
    keep, send = reduce_step(bits, 4, [keep, came], ((0, HALF, HALF),), 32)
    came = swap(send, s4)
    units = [((UNIT, C), I16), ((UNIT, C), I16)]
    if extra:
        (total,) = call(total_body, [((HALF, 16, C), F32)], [keep, came])
        for b in extra:
            total = total + swap(total, b)
        unit_a, unit_b = call(unit_body, units, [total])
    else:
        unit_a, unit_b = call(
            total_unit_body, units, [keep, came], scratch=[pltpu.VMEM((HALF, 16, C), F32)]
        )

    unit_a, unit_b, dy = lax.optimization_barrier((unit_a, unit_b, dy))
    back_args = [got[window // 2 + 1], got[window // 2 - 1], dy_local, ekey, weight]
    back_scratch = [pltpu.VMEM((1, 3, 800, C), BF), pltpu.VMEM((512, C), F32)]
    far = swap(jnp.concatenate([unit_a, unit_b], axis=0), s4)
    (backward,) = call(
        functools.partial(backward_first_body, base=cap + TAIL),
        [((512, C), BF)],
        [dy, *back_args],
        scratch=back_scratch,
        flops=conv_flops // 2,
        moved=5 * MIB,
    )
    far, backward, dy = lax.optimization_barrier((far, backward, dy))
    unit_a = jnp.concatenate([unit_a, far[:UNIT]], axis=0)
    unit_b = jnp.concatenate([unit_b, far[UNIT:]], axis=0)
    far = swap(jnp.concatenate([unit_a, unit_b], axis=0), s3)
    (backward,) = call(
        functools.partial(backward_body, base=cap + TAIL),
        [((rows, C), BF)],
        [dy, *back_args, backward],
        scratch=back_scratch,
        flops=conv_flops // 2,
        moved=5 * MIB,
    )
    far, backward = lax.optimization_barrier((far, backward))
    unit_a = jnp.concatenate([unit_a, far[: 2 * UNIT]], axis=0)
    unit_b = jnp.concatenate([unit_b, far[2 * UNIT :]], axis=0)
    far_a, far_b = swap(unit_a, s2), swap(unit_b, s1)
    unit_a = jnp.concatenate([unit_a, far_a], axis=0)
    unit_b = jnp.concatenate([unit_b, far_b], axis=0)
    far_a, far_b = swap(unit_a, s1), swap(unit_b, s2)
    other_a, other_b = swap(unit_a, s0), swap(unit_b, s0)
    other_far_a, other_far_b = swap(far_a, s0), swap(far_b, s0)
    (weight_grad,) = call(
        finish_body,
        [((27, C, C), BF)],
        [bits, unit_a, far_a, unit_b, far_b, other_a, other_far_a, other_b, other_far_b],
        smem=(0,),
        scratch=[
            pltpu.VMEM((2 * HALF, C, C), BF),
            pltpu.VMEM((2, C, C), BF),
            pltpu.VMEM((64, C), F32),
            pltpu.SemaphoreType.DMA((2 * HALF,)),
        ],
        far_out=True,
    )
    return forward[None], backward[None], weight_grad


def solution(mesh):
    placed = (P("dp", "pts", None), P("dp", "pts"), P(), P("dp", "pts", None), P("dp", "pts", None))
    return jax.shard_map(
        on_device,
        mesh=mesh,
        in_specs=placed,
        out_specs=(P("dp", "pts", None), P("dp", "pts", None), P()),
        check_vma=False,
    )
```
